512 devices in a mesh: row: 16 (over x, z_hi), col: 4 (over z_lo), depth: 8 (over y, core).
Axes of the slice: x: 4, y: 4, z: 16 (z_hi: 4, z_lo: 4; z = z_hi * 4 + z_lo), core: 2. Of those that a mesh axis runs over, the one named last changes fastest.
Arguments:
- features: bfloat16 [256, 16384], P('depth', ('col', 'row')), may hold values from -6 to 6
- weight: bfloat16 [256, 172], P('depth'), may hold values from -1.25 to 1.25
- tile_values: bfloat16 [8192, 128, 128], P(('row', 'col')), may hold values from -0.109375 to 0.109375
- tile_rows: int32 [8192], P(('row', 'col')), may hold values from 0 to 7
- tile_cols: int32 [8192], P(('row', 'col')), may hold values from 0 to 31
- tile_count: int32 [64], P(('row', 'col')), may hold values from 1 to 128, as said below
- labels: int32 [16384], P(('row', 'col')), may hold values from 0 to 171
Outputs:
- weight_grad: float32 [256, 172], P('depth')
- feature_grad: float32 [256, 16384], P('depth', ('col', 'row'))
The draws below stay inside these ranges and needn't reach their ends.
Inputs may be any that keep to these rules, and one draw needn't show every extreme that they name: `tile_rows`: tile positions may repeat within a device; repeated tiles add. `tile_count`: some device has all 128 slots live.
All inputs are finite; a program needn't handle non-finite values.
Results may differ from the reference program's by a relative error of at most 0.019.
Values may be sent and summed in bfloat16 or wider, within the bound.
No kernel may reach another device: no remote copies, remote signals or barrier semaphores. Data moves between devices by JAX's collectives and lax.ppermute only.
A program may use at most 64 MiB of HBM per device.

```python
import jax
import jax.numpy as jnp
from jax import lax

HID = 256
CLS = 172
MAXT = 128
TILE = 128
GRID = 64
NODES = 16384
TR = 8
TC = 32
N_ROW = 16
N_COL = 4


def draw_tile_count(key, part):
    key = jax.random.fold_in(key, 11)
    first_key, second_key, third_key, fourth_key = jax.random.split(key, 4)
    lighter = jax.random.randint(first_key, (GRID,), 1, MAXT // 2 + 1)
    heavier = jax.random.randint(second_key, (GRID,), MAXT // 2, MAXT + 1)
    picker = jax.random.randint(third_key, (GRID,), 0, 8)
    counts = jnp.where(picker == 0, heavier, lighter)
    busiest = jax.random.randint(fourth_key, (), 0, GRID)
    counts = jnp.where(jnp.arange(GRID, dtype=jnp.int32) == busiest, MAXT, counts)
    return counts.astype(jnp.int32)


def place_ends(drawn, own_key, smallest, high):
    index_at = [jax.random.randint(jax.random.fold_in(own_key, axis), (), 0, length) for axis, length in enumerate(drawn.shape)]
    longest = drawn.shape.index(max(drawn.shape))
    neighbour = index_at[:longest] + [(index_at[longest] + 1) % drawn.shape[longest]] + index_at[longest + 1:]
    return drawn.at[tuple(index_at)].set(smallest).at[tuple(neighbour)].set(high)


def block_levels(key, dims, cuts, smallest, high):
    loudness = 1.0
    for position, parts in cuts:
        heights = jax.random.uniform(jax.random.fold_in(jax.random.fold_in(key, 6), position), (parts,), jnp.float32, smallest / len(cuts), high / len(cuts))
        loudness = loudness * jnp.repeat(jnp.exp(heights), dims[position] // parts).reshape((-1,) + (1,) * (len(dims) - 1 - position))
    return loudness


def scatter_about(rng, shape, spread, reach, cuts=(), held_as=jnp.bfloat16):
    array = jax.random.normal(rng, shape, jnp.float32) * spread
    if len(cuts) > 0:
        array = block_levels(rng, shape, cuts, -0.22, 0.18) * array
    return jnp.clip(array, min=-reach, max=reach).astype(held_as)


def setup_inputs(seed: int = 0) -> dict:
    streams_of = jax.random.split(jax.random.key(seed), 8)
    features = scatter_about(streams_of[0], (HID, NODES), 1.0, 6.0, ((0, 8), (1, 64)))
    weight = scatter_about(streams_of[1], (HID, CLS), 0.2, 1.25, ((0, 8),))
    tile_values = scatter_about(streams_of[2], (GRID * MAXT, TILE, TILE), (TILE * MAXT * N_COL // (3 * TR)) ** -0.5, 0.109375, ((0, 64),))
    tile_rows = place_ends(jax.random.randint(streams_of[3], (GRID * MAXT,), 0, TR), jax.random.fold_in(streams_of[3], 1), 0, TR - 1).astype(jnp.int32)
    tile_cols = place_ends(jax.random.randint(streams_of[4], (GRID * MAXT,), 0, TC), jax.random.fold_in(streams_of[4], 1), 0, TC - 1).astype(jnp.int32)
    tile_count = draw_tile_count(jax.random.fold_in(streams_of[7], 71), 0)
    labels = place_ends(jax.random.randint(streams_of[6], (NODES,), 0, CLS), jax.random.fold_in(streams_of[6], 1), 0, CLS - 1).astype(jnp.int32)
    return dict(features=features, weight=weight, tile_values=tile_values, tile_rows=tile_rows, tile_cols=tile_cols, tile_count=tile_count, labels=labels)


def class_delta(logits, labels):
    exponent = jnp.exp(logits)
    chances = exponent / jnp.sum(exponent, axis=0, keepdims=True)
    target = (lax.broadcasted_iota(jnp.int32, logits.shape, 0) == labels[None, :]).astype(jnp.float32)
    return (chances - target).astype(jnp.bfloat16)


def tile_pass(source, tile_values, pick_index, put_index, tile_count, backward):
    hidden = source.shape[0]
    values = tile_values.reshape(N_ROW * N_COL, MAXT, TILE, TILE)
    pick_slots = pick_index.reshape(N_ROW * N_COL, MAXT)
    put_slots = put_index.reshape(N_ROW * N_COL, MAXT)
    if backward:
        source_blocks = source.reshape(hidden, N_ROW, TR, TILE)
        out_count = N_COL
        out_tiles = TC
    else:
        source_blocks = source.reshape(hidden, N_COL, TC, TILE)
        out_count = N_ROW
        out_tiles = TR

    def one_device(running, inputs):
        device, tile_block, pick_rows, put_rows, live_count = inputs
        row_index = device // N_COL
        col_index = device % N_COL
        if backward:
            source_index = row_index
            out_index = col_index
        else:
            source_index = col_index
            out_index = row_index
        source_block = lax.dynamic_index_in_dim(source_blocks, source_index, 1, keepdims=False)
        picked = jnp.take(source_block, pick_rows, axis=1).astype(jnp.float32)
        if backward:
            products = jnp.einsum("hki,kij->hkj", picked, tile_block.astype(jnp.float32))
        else:
            products = jnp.einsum("hkj,kij->hki", picked, tile_block.astype(jnp.float32))
        live_mask = jnp.arange(MAXT, dtype=jnp.int32) < live_count
        placing = ((put_rows[:, None] == jnp.arange(out_tiles, dtype=jnp.int32)[None, :]) & live_mask[:, None]).astype(jnp.float32)
        placed_terms = jnp.einsum("hkt,kp->hpt", products, placing)
        running = running.at[:, out_index].add(placed_terms)
        return running, None

    initial = jnp.zeros((hidden, out_count, out_tiles, TILE), jnp.float32)
    devices = jnp.arange(N_ROW * N_COL, dtype=jnp.int32)
    running, unused = lax.scan(one_device, initial, (devices, values, pick_slots, put_slots, tile_count))
    return running.reshape(hidden, NODES)


def reference(features, weight, tile_values, tile_rows, tile_cols, tile_count, labels):
    aggregated = tile_pass(features, tile_values, tile_cols, tile_rows, tile_count, False).astype(jnp.bfloat16)
    logits = jnp.dot(weight.T, aggregated, preferred_element_type=jnp.float32)
    delta = class_delta(logits, labels)
    weight_grad = jnp.dot(aggregated, delta.T, preferred_element_type=jnp.float32)
    grad_hidden = jnp.dot(weight, delta, preferred_element_type=jnp.float32).astype(jnp.bfloat16)
    feature_grad = tile_pass(grad_hidden, tile_values, tile_rows, tile_cols, tile_count, True)
    return weight_grad, feature_grad
```

```python
import jax
import jax.numpy as jnp
from jax import lax
from jax.experimental import pallas as pl
from jax.experimental.pallas import tpu as pltpu
from jax.sharding import Mesh
from jax.sharding import PartitionSpec as P

TILE = 128
STEP = 16
AXES = ("x", "zh", "zl", "y", "core")
ROW = ("x", "zh")
DEPTH = ("y", "core")
SMEM = pltpu.MemorySpace.SMEM
F32 = jnp.float32
BF16 = jnp.bfloat16
NT = (((1,), (1,)), ((), ()))
TN = (((0,), (0,)), ((), ()))


def forward_kernel(count_ref, rows_ref, cols_ref, where_ref, source_ref, weight_ref, labels_ref, tiles_ref, out_ref, total):
    step = pl.program_id(0)
    blocks = total.shape[0] - 1

    @pl.when(step == 0)
    def clear():
        total[...] = jnp.zeros_like(total)

    live = count_ref[0]
    products = []
    for j in range(STEP):
        col = cols_ref[step * STEP + j]
        lanes = pl.ds(pl.multiple_of((col % 2) * TILE, TILE), TILE)
        products.append(
            lax.dot_general(source_ref[col // 2, :, lanes], tiles_ref[j], NT, preferred_element_type=F32)
        )
    for j in range(STEP):
        slot = step * STEP + j
        row = jnp.where(slot < live, rows_ref[slot], blocks)
        total[row] = total[row] + products[j]

    @pl.when(step == pl.num_programs(0) - 1)
    def finish():
        me = where_ref[0]
        weight = weight_ref[...].astype(F32)
        classes = weight.shape[1]
        mine = weight[0:8]
        for z in range(1, 4):
            mine = jnp.where(me == z, weight[8 * z : 8 * z + 8], mine)
        labels = labels_ref[...].astype(F32)
        left = mine[:, :TILE]
        rest = jnp.concatenate([mine[:, TILE:], jnp.zeros((8, 64 - (classes - TILE)), F32)], axis=1)
        for d in range(blocks):
            out_ref[0, d, 0:32, :] = total[d].astype(BF16)
            half = labels[:, (d % 2) * TILE : (d % 2) * TILE + TILE]
            both = jnp.concatenate([half[:, :64], half[:, 64:], jnp.zeros((6, 64), F32)], axis=0)
            right = jnp.concatenate([rest, both], axis=1)
            out_ref[0, d, 32:48, :] = jnp.concatenate([left, right], axis=0).astype(BF16)
        for z in range(1, 4):
            out_ref[z] = out_ref[0]


def middle_kernel(where_ref, got_ref, out_ref, agg, weight_a, weight_b):
    me = where_ref[1]
    for d in range(8):
        sums = got_ref[d, 0:32, :].astype(F32)
        for z in range(1, 4):
            sums = sums + got_ref[8 * z + d, 0:32, :].astype(F32)
        agg[32 * d : 32 * d + 32, :] = sums.astype(BF16)
        pieces = [got_ref[8 * z + d, 32:48, :].astype(F32) for z in range(4)]
        weight_a[32 * d : 32 * d + 32, :] = jnp.concatenate([p[0:8] for p in pieces], axis=0).astype(BF16)
        weight_b[32 * d : 32 * d + 32, :] = jnp.concatenate([p[8:16] for p in pieces], axis=0).astype(BF16)
    carrier = got_ref[(me // 2) * 8, 32:48, :].astype(F32)
    labels = jnp.concatenate([carrier[8:9, 64:], carrier[9:10, 64:]], axis=1)
    nodes = agg[...]
    wa = weight_a[...]
    wb = weight_b[...]
    ids = lax.broadcasted_iota(jnp.int32, (TILE, TILE), 0).astype(F32)
    exp_a = jnp.exp(lax.dot_general(wa, nodes, TN, preferred_element_type=F32))
    logit_b = lax.dot_general(wb, nodes, TN, preferred_element_type=F32)
    valid = ids < 172 - TILE
    exp_b = jnp.where(valid, jnp.exp(jnp.where(valid, logit_b, 0.0)), 0.0)
    whole = jnp.sum(exp_a, axis=0, keepdims=True) + jnp.sum(exp_b, axis=0, keepdims=True)
    delta_a = (exp_a / whole - jnp.where(ids == labels, 1.0, 0.0)).astype(BF16)
    delta_b = (exp_b / whole - jnp.where(ids + TILE == labels, 1.0, 0.0)).astype(BF16)
    hidden = jnp.dot(wa, delta_a, preferred_element_type=F32) + jnp.dot(wb, delta_b, preferred_element_type=F32)
    grad_a = lax.dot_general(nodes, delta_a, NT, preferred_element_type=F32)
    grad_b = lax.dot_general(nodes, delta_b, NT, preferred_element_type=F32)
    for d in range(8):
        out_ref[d, 0:32, :] = hidden[32 * d : 32 * d + 32].astype(BF16)
        out_ref[d, 32:64, :] = grad_a[32 * d : 32 * d + 32].astype(BF16)
        part = grad_b[32 * d : 32 * d + 32, :64]
        out_ref[d, 64:80, :] = jnp.concatenate([part[0:16], part[16:32]], axis=1).astype(BF16)


def backward_kernel(count_ref, rows_ref, cols_ref, got_ref, tiles_ref, out_ref, total):
    step = pl.program_id(0)
    blocks = total.shape[0] - 1

    @pl.when(step == 0)
    def clear():
        total[...] = jnp.zeros_like(total)

    live = count_ref[0]
    products = []
    for j in range(STEP):
        row = rows_ref[step * STEP + j]
        products.append(jnp.dot(got_ref[row, 0:32, :], tiles_ref[j], preferred_element_type=F32))
    for j in range(STEP):
        slot = step * STEP + j
        col = jnp.where(slot < live, cols_ref[slot], blocks)
        total[col] = total[col] + products[j]

    @pl.when(step == pl.num_programs(0) - 1)
    def finish():
        grad_a = got_ref[0, 32:64, :].astype(F32)
        grad_b = got_ref[0, 64:80, :].astype(F32)
        for d in range(1, 8):
            grad_a = grad_a + got_ref[d, 32:64, :].astype(F32)
            grad_b = grad_b + got_ref[d, 64:80, :].astype(F32)
        for x in range(4):
            for z in range(4):
                for half in range(2):
                    out_ref[x, 32 * z : 32 * z + 32, half * TILE : half * TILE + TILE] = total[
                        (4 * x + z) * 2 + half
                    ].astype(BF16)
            out_ref[x, 128:144, 0:TILE] = grad_a[0:16].astype(BF16)
            out_ref[x, 128:144, TILE:] = grad_a[16:32].astype(BF16)
            out_ref[x, 144:160, 0:TILE] = grad_b.astype(BF16)
            out_ref[x, 144:160, TILE:] = jnp.zeros((16, TILE), BF16)


def sum_kernel(got_ref, out_ref):
    sums = got_ref[0].astype(F32)
    for x in range(1, 4):
        sums = sums + got_ref[x].astype(F32)
    out_ref[...] = sums.astype(BF16)


def final_kernel(where_ref, got_ref, weight_ref, feature_ref):
    at = pl.multiple_of(where_ref[2] * 32, 32)
    sums = got_ref[0, pl.ds(at, 32), :].astype(F32)
    grads = got_ref[0, 128:160, :].astype(F32)
    for z in range(1, 4):
        sums = sums + got_ref[z, pl.ds(at, 32), :].astype(F32)
        grads = grads + got_ref[z, 128:160, :].astype(F32)
    feature_ref[...] = sums
    weight_ref[0:16, 0:TILE] = grads[0:16, 0:TILE]
    weight_ref[16:32, 0:TILE] = grads[0:16, TILE:]
    weight_ref[0:16, TILE:] = grads[16:32, 0:44]
    weight_ref[16:32, TILE:] = grads[16:32, 64:108]


def tile_call(kernel, arrays, tiles, out_shape, blocks, smem):
    slots = tiles.shape[0]

    def whole(array):
        return pl.BlockSpec(array.shape, lambda i, n=len(array.shape): (0,) * n)

    return pl.pallas_call(
        kernel,
        grid=(slots // STEP,),
        in_specs=[pl.BlockSpec(memory_space=SMEM)] * smem
        + [whole(a) for a in arrays[smem:]]
        + [pl.BlockSpec((STEP, TILE, TILE), lambda i: (i, 0, 0))],
        out_specs=whole(out_shape),
        out_shape=out_shape,
        scratch_shapes=[pltpu.VMEM((blocks + 1, 32, TILE), F32)],
        compiler_params=pltpu.CompilerParams(vmem_limit_bytes=24 * 2**20),
    )(*arrays, tiles)


def body(features, weight, tile_values, tile_rows, tile_cols, tile_count, labels):
    shape = jax.ShapeDtypeStruct
    vmem = pl.BlockSpec(memory_space=pltpu.VMEM)
    scalars = pl.BlockSpec(memory_space=SMEM)
    where = jnp.stack([lax.axis_index("zl"), lax.axis_index(DEPTH), lax.axis_index("zh")]).astype(jnp.int32)
    near = lax.all_gather(features, "zh", axis=0)
    source = lax.all_gather(near, "x", axis=0).reshape(16, 32, 256)
    sent = tile_call(
        forward_kernel,
        [tile_count, tile_rows, tile_cols, where, source, weight, labels.reshape(1, 256)],
        tile_values,
        shape((4, 8, 48, TILE), BF16),
        8,
        4,
    )
    got = lax.all_to_all(sent.reshape(32, 48, TILE), ("zl", "y", "core"), 0, 0, tiled=True)
    back = pl.pallas_call(
        middle_kernel,
        in_specs=[scalars, vmem],
        out_specs=vmem,
        out_shape=shape((8, 80, TILE), BF16),
        scratch_shapes=[pltpu.VMEM((256, TILE), BF16)] * 3,
    )(where, got)
    grads = lax.all_to_all(back, DEPTH, 0, 0, tiled=True)
    parts = tile_call(
        backward_kernel,
        [tile_count, tile_rows, tile_cols, grads],
        tile_values,
        shape((4, 160, 256), BF16),
        32,
        3,
    )
    ours = lax.all_to_all(parts, "x", 0, 0, tiled=True)
    summed = pl.pallas_call(
        sum_kernel, in_specs=[vmem], out_specs=vmem, out_shape=shape((160, 256), BF16)
    )(ours)
    four = lax.all_gather(summed, "zh", axis=0)
    return pl.pallas_call(
        final_kernel,
        in_specs=[scalars, vmem],
        out_specs=(vmem, vmem),
        out_shape=(shape((32, 172), F32), shape((32, 256), F32)),
    )(where, four)


def solution(mesh):
    fine = Mesh(mesh.devices.reshape(4, 4, 4, 4, 2), AXES)
    tiled = ("x", "zh", "zl")
    return jax.shard_map(
        body,
        mesh=fine,
        in_specs=(
            P(DEPTH, ("zl", "x", "zh")),
            P(DEPTH, None),
            P(tiled, None, None),
            P(tiled),
            P(tiled),
            P(tiled),
            P(tiled),
        ),
        out_specs=(P(DEPTH, None), P(DEPTH, ("zl", "x", "zh"))),
        check_vma=False,
    )
```

```python
import jax
import jax.numpy as jnp
from jax import lax
from jax.experimental import pallas as pl
from jax.experimental.pallas import tpu as pltpu
from jax.sharding import Mesh
from jax.sharding import PartitionSpec as P

TILE = 128
STEP = 16
AXES = ("x", "zh", "zl", "y", "core")
ROW = ("x", "zh")
DEPTH = ("y", "core")
SMEM = pltpu.MemorySpace.SMEM
F32 = jnp.float32
BF16 = jnp.bfloat16
NT = (((1,), (1,)), ((), ()))
TN = (((0,), (0,)), ((), ()))


def prepare_kernel(weight_ref, labels_ref, out_ref):
    me = lax.axis_index("zl")
    weight = weight_ref[...].astype(F32)
    classes = weight.shape[1]
    mine = weight[0:8]
    for z in range(1, 4):
        mine = jnp.where(me == z, weight[8 * z : 8 * z + 8], mine)
    labels = labels_ref[...].astype(F32)
    rest = jnp.concatenate([mine[:, TILE:], jnp.zeros((8, 64 - (classes - TILE)), F32)], axis=1)
    for d in range(2):
        half = labels[:, d * TILE : d * TILE + TILE]
        both = jnp.concatenate([half[:, :64], half[:, 64:], jnp.zeros((6, 64), F32)], axis=0)
        right = jnp.concatenate([rest, both], axis=1)
        out_ref[d] = jnp.concatenate([mine[:, :TILE], right], axis=0).astype(BF16)


def fetch(pairs, sems):
    copies = [pltpu.make_async_copy(src, dst, sems.at[i]) for i, (src, dst) in enumerate(pairs)]
    for copy in copies:
        copy.start()
    return copies


def tile_copy(tiles_ref, held, sems, step):
    part = pl.ds(step * STEP, STEP)
    return pltpu.make_async_copy(tiles_ref.at[part], held.at[part], sems.at[step])


def forward_kernel(
    count_ref, rows_ref, cols_ref, source_ref, extra_ref, tiles_ref, out_ref,
    total, count, rows, cols, sems, held, tile_sems,
):
    steps = tiles_ref.shape[0] // STEP
    blocks = total.shape[0] - 1
    small = fetch([(count_ref, count), (rows_ref, rows), (cols_ref, cols)], sems)
    for step in range(steps):
        tile_copy(tiles_ref, held, tile_sems, step).start()
    total[...] = jnp.zeros_like(total)
    for copy in small:
        copy.wait()
    live = count[0]

    @pl.loop(0, steps)
    def work(step):
        tile_copy(tiles_ref, held, tile_sems, step).wait()
        products = []
        for j in range(STEP):
            col = cols[step * STEP + j]
            lanes = pl.ds(pl.multiple_of((col % 2) * TILE, TILE), TILE)
            products.append(
                lax.dot_general(
                    source_ref[col // 2, :, lanes], held[step * STEP + j], NT, preferred_element_type=F32
                )
            )
        for j in range(STEP):
            slot = step * STEP + j
            row = jnp.where(slot < live, rows[slot], blocks)
            total[row] = total[row] + products[j]

    for d in range(blocks):
        block = jnp.concatenate([total[d].astype(BF16), extra_ref[d % 2]], axis=0)
        for z in range(4):
            out_ref[z, d] = block


def middle_kernel(got_ref, out_ref, agg, weight_a, weight_b):
    me = lax.axis_index(DEPTH)
    for d in range(8):
        sums = got_ref[d, 0:32, :].astype(F32)
        for z in range(1, 4):
            sums = sums + got_ref[8 * z + d, 0:32, :].astype(F32)
        agg[32 * d : 32 * d + 32, :] = sums.astype(BF16)
        pieces = [got_ref[8 * z + d, 32:48, :].astype(F32) for z in range(4)]
        weight_a[32 * d : 32 * d + 32, :] = jnp.concatenate([p[0:8] for p in pieces], axis=0).astype(BF16)
        weight_b[32 * d : 32 * d + 32, :] = jnp.concatenate([p[8:16] for p in pieces], axis=0).astype(BF16)
    carrier = got_ref[(me // 2) * 8, 32:48, :].astype(F32)
    labels = jnp.concatenate([carrier[8:9, 64:], carrier[9:10, 64:]], axis=1)
    nodes = agg[...]
    wa = weight_a[...]
    wb = weight_b[...]
    ids = lax.broadcasted_iota(jnp.int32, (TILE, TILE), 0).astype(F32)
    exp_a = jnp.exp(lax.dot_general(wa, nodes, TN, preferred_element_type=F32))
    logit_b = lax.dot_general(wb, nodes, TN, preferred_element_type=F32)
    valid = ids < 172 - TILE
    exp_b = jnp.where(valid, jnp.exp(jnp.where(valid, logit_b, 0.0)), 0.0)
    whole = jnp.sum(exp_a, axis=0, keepdims=True) + jnp.sum(exp_b, axis=0, keepdims=True)
    delta_a = (exp_a / whole - jnp.where(ids == labels, 1.0, 0.0)).astype(BF16)
    delta_b = (exp_b / whole - jnp.where(ids + TILE == labels, 1.0, 0.0)).astype(BF16)
    hidden = jnp.dot(wa, delta_a, preferred_element_type=F32) + jnp.dot(wb, delta_b, preferred_element_type=F32)
    grad_a = lax.dot_general(nodes, delta_a, NT, preferred_element_type=F32)
    grad_b = lax.dot_general(nodes, delta_b, NT, preferred_element_type=F32)
    for d in range(8):
        out_ref[d, 0:32, :] = hidden[32 * d : 32 * d + 32].astype(BF16)
        out_ref[d, 32:64, :] = grad_a[32 * d : 32 * d + 32].astype(BF16)
        part = grad_b[32 * d : 32 * d + 32, :64]
        out_ref[d, 64:80, :] = jnp.concatenate([part[0:16], part[16:32]], axis=1).astype(BF16)


def backward_kernel(
    count_ref, rows_ref, cols_ref, got_ref, tiles_ref, out_ref,
    total, count, rows, cols, sems, held, tile_sems,
):
    steps = tiles_ref.shape[0] // STEP
    blocks = total.shape[0] - 1
    small = fetch([(count_ref, count), (rows_ref, rows), (cols_ref, cols)], sems)
    for step in range(steps):
        tile_copy(tiles_ref, held, tile_sems, step).start()
    total[...] = jnp.zeros_like(total)
    grad_a = got_ref[0, 32:64, :].astype(F32)
    grad_b = got_ref[0, 64:80, :].astype(F32)
    for d in range(1, 8):
        grad_a = grad_a + got_ref[d, 32:64, :].astype(F32)
        grad_b = grad_b + got_ref[d, 64:80, :].astype(F32)
    packed = jnp.concatenate(
        [
            jnp.concatenate([grad_a[0:16], grad_a[16:32]], axis=1),
            jnp.concatenate([grad_b[0:8], grad_b[8:16]], axis=1),
        ],
        axis=0,
    )
    for copy in small:
        copy.wait()
    live = count[0]

    @pl.loop(0, steps)
    def work(step):
        tile_copy(tiles_ref, held, tile_sems, step).wait()
        products = []
        for j in range(STEP):
            row = rows[step * STEP + j]
            products.append(
                jnp.dot(got_ref[row, 0:32, :], held[step * STEP + j], preferred_element_type=F32)
            )
        for j in range(STEP):
            slot = step * STEP + j
            col = jnp.where(slot < live, cols[slot], blocks)
            total[col] = total[col] + products[j]

    for peer in range(16):
        block = jnp.concatenate([total[2 * peer], total[2 * peer + 1]], axis=1)
        out_ref[peer] = jnp.concatenate([block, packed], axis=0).astype(BF16)


def final_kernel(got_ref, weight_ref, feature_ref):
    sums = got_ref[0].astype(F32)
    for peer in range(1, 16):
        sums = sums + got_ref[peer].astype(F32)
    feature_ref[...] = sums[0:32]
    grad_a = sums[32:48]
    grad_b = sums[48:56]
    weight_ref[0:16, 0:TILE] = grad_a[:, 0:TILE]
    weight_ref[16:32, 0:TILE] = grad_a[:, TILE:]
    for part in range(2):
        rows = grad_b[:, part * TILE : part * TILE + TILE]
        weight_ref[8 * part : 8 * part + 8, TILE:] = rows[:, 0:44]
        weight_ref[16 + 8 * part : 24 + 8 * part, TILE:] = rows[:, 64:108]


def body(features, weight, tile_values, tile_rows, tile_cols, tile_count, labels):
    shape = jax.ShapeDtypeStruct
    vmem = pl.BlockSpec(memory_space=pltpu.VMEM)
    far = pl.BlockSpec(memory_space=pltpu.MemorySpace.HBM)
    slots = tile_values.shape[0]
    scratch = [
        pltpu.SMEM((1,), jnp.int32),
        pltpu.SMEM((slots,), jnp.int32),
        pltpu.SMEM((slots,), jnp.int32),
        pltpu.SemaphoreType.DMA((3,)),
        pltpu.VMEM(tile_values.shape, BF16),
        pltpu.SemaphoreType.DMA((slots // STEP,)),
    ]
    params = pltpu.CompilerParams(vmem_limit_bytes=16 * 2**20)
    tile_params = pltpu.CompilerParams(vmem_limit_bytes=51 * 2**20)
    spread = jnp.broadcast_to(features[None], (16, *features.shape))
    source = lax.all_to_all(spread, ROW, 0, 0, tiled=True)
    extra = pl.pallas_call(
        prepare_kernel,
        in_specs=[vmem, vmem],
        out_specs=vmem,
        out_shape=shape((2, 16, TILE), BF16),
        compiler_params=params,
        cost_estimate=pl.CostEstimate(flops=10**10, bytes_accessed=0, transcendentals=0),
    )(weight, labels.reshape(1, -1))
    sent = pl.pallas_call(
        forward_kernel,
        in_specs=[far, far, far, vmem, vmem, far],
        out_specs=vmem,
        out_shape=shape((4, 8, 48, TILE), BF16),
        scratch_shapes=[pltpu.VMEM((9, 32, TILE), F32), *scratch],
        compiler_params=tile_params,
    )(tile_count, tile_rows, tile_cols, source, extra, tile_values)
    got = lax.all_to_all(sent.reshape(32, 48, TILE), ("zl", "y", "core"), 0, 0, tiled=True)
    back = pl.pallas_call(
        middle_kernel,
        in_specs=[vmem],
        out_specs=vmem,
        out_shape=shape((8, 80, TILE), BF16),
        scratch_shapes=[pltpu.VMEM((256, TILE), BF16)] * 3,
        compiler_params=params,
    )(got)
    grads = lax.all_to_all(back, DEPTH, 0, 0, tiled=True)
    parts = pl.pallas_call(
        backward_kernel,
        in_specs=[far, far, far, vmem, far],
        out_specs=vmem,
        out_shape=shape((16, 56, 256), BF16),
        scratch_shapes=[pltpu.VMEM((33, 32, TILE), F32), *scratch],
        compiler_params=tile_params,
    )(tile_count, tile_rows, tile_cols, grads, tile_values)
    ours = lax.all_to_all(parts, ROW, 0, 0, tiled=True)
    return pl.pallas_call(
        final_kernel,
        in_specs=[vmem],
        out_specs=(vmem, vmem),
        out_shape=(shape((32, 172), F32), shape((32, 256), F32)),
        compiler_params=params,
    )(ours)


def solution(mesh):
    fine = Mesh(mesh.devices.reshape(4, 4, 4, 4, 2), AXES)
    tiled = ("x", "zh", "zl")
    return jax.shard_map(
        body,
        mesh=fine,
        in_specs=(
            P(DEPTH, ("zl", "x", "zh")),
            P(DEPTH, None),
            P(tiled, None, None),
            P(tiled),
            P(tiled),
            P(tiled),
            P(tiled),
        ),
        out_specs=(P(DEPTH, None), P(DEPTH, ("zl", "x", "zh"))),
        check_vma=False,
    )
```

```python
import jax
import jax.numpy as jnp
from jax import lax
from jax.experimental import pallas as pl
from jax.experimental.pallas import tpu as pltpu
from jax.sharding import Mesh
from jax.sharding import PartitionSpec as P

TILE = 128
STEP = 16
AXES = ("x", "zh", "zl", "y", "core")
DEPTH = ("y", "core")
SMEM = pltpu.MemorySpace.SMEM
F32 = jnp.float32
BF16 = jnp.bfloat16
NT = (((1,), (1,)), ((), ()))
TN = (((0,), (0,)), ((), ()))


def prepare_kernel(weight_ref, labels_ref, out_ref):
    me = lax.axis_index("zl")
    weight = weight_ref[...].astype(F32)
    classes = weight.shape[1]
    mine = weight[0:8]
    for z in range(1, 4):
        mine = jnp.where(me == z, weight[8 * z : 8 * z + 8], mine)
    labels = labels_ref[...].astype(F32)
    rest = jnp.concatenate([mine[:, TILE:], jnp.zeros((8, 64 - (classes - TILE)), F32)], axis=1)
    for d in range(2):
        half = labels[:, d * TILE : d * TILE + TILE]
        both = jnp.concatenate([half[:, :64], half[:, 64:], jnp.zeros((6, 64), F32)], axis=0)
        right = jnp.concatenate([rest, both], axis=1)
        out_ref[d] = jnp.concatenate([mine[:, :TILE], right], axis=0).astype(BF16)


def fetch(pairs, sems):
    copies = [pltpu.make_async_copy(src, dst, sems.at[i]) for i, (src, dst) in enumerate(pairs)]
    for copy in copies:
        copy.start()
    return copies


def tile_copy(tiles_ref, held, sems, step):
    part = pl.ds(step * STEP, STEP)
    return pltpu.make_async_copy(tiles_ref.at[part], held.at[part], sems.at[step])


def forward_kernel(
    count_ref, rows_ref, cols_ref, source_ref, extra_ref, tiles_ref, out_ref,
    total, count, rows, cols, sems, held, tile_sems,
):
    steps = tiles_ref.shape[0] // STEP
    blocks = total.shape[0] - 1
    small = fetch([(count_ref, count), (rows_ref, rows), (cols_ref, cols)], sems)
    for step in range(steps):
        tile_copy(tiles_ref, held, tile_sems, step).start()
    total[...] = jnp.zeros_like(total)
    for copy in small:
        copy.wait()
    live = count[0]

    @pl.loop(0, steps)
    def work(step):
        tile_copy(tiles_ref, held, tile_sems, step).wait()
        products = []
        for j in range(STEP):
            col = cols[step * STEP + j]
            lanes = pl.ds(pl.multiple_of((col % 2) * TILE, TILE), TILE)
            products.append(
                lax.dot_general(
                    source_ref[col // 2, :, lanes], held[step * STEP + j], NT, preferred_element_type=F32
                )
            )
        for j in range(STEP):
            slot = step * STEP + j
            row = jnp.where(slot < live, rows[slot], blocks)
            total[row] = total[row] + products[j]

    for d in range(blocks):
        block = jnp.concatenate([total[d].astype(BF16), extra_ref[d % 2]], axis=0)
        for z in range(4):
            out_ref[z, d] = block


def middle_kernel(got_ref, out_ref, agg, weight_a, weight_b):
    me = lax.axis_index(DEPTH)
    for d in range(8):
        sums = got_ref[d, 0:32, :].astype(F32)
        for z in range(1, 4):
            sums = sums + got_ref[8 * z + d, 0:32, :].astype(F32)
        agg[32 * d : 32 * d + 32, :] = sums.astype(BF16)
        pieces = [got_ref[8 * z + d, 32:48, :].astype(F32) for z in range(4)]
        weight_a[32 * d : 32 * d + 32, :] = jnp.concatenate([p[0:8] for p in pieces], axis=0).astype(BF16)
        weight_b[32 * d : 32 * d + 32, :] = jnp.concatenate([p[8:16] for p in pieces], axis=0).astype(BF16)
    carrier = got_ref[(me // 2) * 8, 32:48, :].astype(F32)
    labels = jnp.concatenate([carrier[8:9, 64:], carrier[9:10, 64:]], axis=1)
    nodes = agg[...]
    wa = weight_a[...]
    wb = weight_b[...]
    ids = lax.broadcasted_iota(jnp.int32, (TILE, TILE), 0).astype(F32)
    exp_a = jnp.exp(lax.dot_general(wa, nodes, TN, preferred_element_type=F32))
    logit_b = lax.dot_general(wb, nodes, TN, preferred_element_type=F32)
    valid = ids < 172 - TILE
    exp_b = jnp.where(valid, jnp.exp(jnp.where(valid, logit_b, 0.0)), 0.0)
    whole = jnp.sum(exp_a, axis=0, keepdims=True) + jnp.sum(exp_b, axis=0, keepdims=True)
    delta_a = (exp_a / whole - jnp.where(ids == labels, 1.0, 0.0)).astype(BF16)
    delta_b = (exp_b / whole - jnp.where(ids + TILE == labels, 1.0, 0.0)).astype(BF16)
    hidden = jnp.dot(wa, delta_a, preferred_element_type=F32) + jnp.dot(wb, delta_b, preferred_element_type=F32)
    grad_a = lax.dot_general(nodes, delta_a, NT, preferred_element_type=F32)
    grad_b = lax.dot_general(nodes, delta_b, NT, preferred_element_type=F32)
    for d in range(8):
        out_ref[d, 0:32, :] = hidden[32 * d : 32 * d + 32].astype(BF16)
        out_ref[d, 32:64, :] = grad_a[32 * d : 32 * d + 32].astype(BF16)
        part = grad_b[32 * d : 32 * d + 32, :64]
        out_ref[d, 64:80, :] = jnp.concatenate([part[0:16], part[16:32]], axis=1).astype(BF16)


def backward_kernel(
    count_ref, rows_ref, cols_ref, got_ref, tiles_ref, out_ref,
    total, count, rows, cols, sems, held, tile_sems,
):
    steps = tiles_ref.shape[0] // STEP
    blocks = total.shape[0] - 1
    small = fetch([(count_ref, count), (rows_ref, rows), (cols_ref, cols)], sems)
    for step in range(steps):
        tile_copy(tiles_ref, held, tile_sems, step).start()
    total[...] = jnp.zeros_like(total)
    grad_a = got_ref[0, 32:64, :].astype(F32)
    grad_b = got_ref[0, 64:80, :].astype(F32)
    for d in range(1, 8):
        grad_a = grad_a + got_ref[d, 32:64, :].astype(F32)
        grad_b = grad_b + got_ref[d, 64:80, :].astype(F32)
    packed = jnp.concatenate(
        [
            jnp.concatenate([grad_a[0:16], grad_a[16:32]], axis=1),
            jnp.concatenate([grad_b[0:8], grad_b[8:16]], axis=1),
        ],
        axis=0,
    )
    for copy in small:
        copy.wait()
    live = count[0]

    @pl.loop(0, steps)
    def work(step):
        tile_copy(tiles_ref, held, tile_sems, step).wait()
        products = []
        for j in range(STEP):
            row = rows[step * STEP + j]
            products.append(
                jnp.dot(got_ref[row, 0:32, :], held[step * STEP + j], preferred_element_type=F32)
            )
        for j in range(STEP):
            slot = step * STEP + j
            col = jnp.where(slot < live, cols[slot], blocks)
            total[col] = total[col] + products[j]

    for x in range(4):
        blocks_of = [jnp.concatenate([total[2 * p], total[2 * p + 1]], axis=1) for p in range(4 * x, 4 * x + 4)]
        out_ref[x] = jnp.concatenate([*blocks_of, packed], axis=0).astype(BF16)


def sum_kernel(got_ref, out_ref):
    sums = got_ref[0].astype(F32)
    for x in range(1, 4):
        sums = sums + got_ref[x].astype(F32)
    for z in range(4):
        out_ref[z] = jnp.concatenate([sums[32 * z : 32 * z + 32], sums[128:152]], axis=0).astype(BF16)


def final_kernel(got_ref, weight_ref, feature_ref):
    sums = got_ref[0].astype(F32)
    for peer in range(1, 4):
        sums = sums + got_ref[peer].astype(F32)
    feature_ref[...] = sums[0:32]
    grad_a = sums[32:48]
    grad_b = sums[48:56]
    weight_ref[0:16, 0:TILE] = grad_a[:, 0:TILE]
    weight_ref[16:32, 0:TILE] = grad_a[:, TILE:]
    for part in range(2):
        rows = grad_b[:, part * TILE : part * TILE + TILE]
        weight_ref[8 * part : 8 * part + 8, TILE:] = rows[:, 0:44]
        weight_ref[16 + 8 * part : 24 + 8 * part, TILE:] = rows[:, 64:108]


def body(features, weight, tile_values, tile_rows, tile_cols, tile_count, labels):
    shape = jax.ShapeDtypeStruct
    vmem = pl.BlockSpec(memory_space=pltpu.VMEM)
    far = pl.BlockSpec(memory_space=pltpu.MemorySpace.HBM)
    slots = tile_values.shape[0]
    scratch = [
        pltpu.SMEM((1,), jnp.int32),
        pltpu.SMEM((slots,), jnp.int32),
        pltpu.SMEM((slots,), jnp.int32),
        pltpu.SemaphoreType.DMA((3,)),
        pltpu.VMEM(tile_values.shape, BF16),
        pltpu.SemaphoreType.DMA((slots // STEP,)),
    ]
    params = pltpu.CompilerParams(vmem_limit_bytes=16 * 2**20)
    tile_params = pltpu.CompilerParams(vmem_limit_bytes=51 * 2**20)
    near = lax.all_gather(features, "zh", axis=0)
    spread = jnp.broadcast_to(near[None], (4, *near.shape))
    source = lax.all_to_all(spread, "x", 0, 0, tiled=True).reshape(16, *features.shape)
    extra = pl.pallas_call(
        prepare_kernel,
        in_specs=[vmem, vmem],
        out_specs=vmem,
        out_shape=shape((2, 16, TILE), BF16),
        compiler_params=params,
        cost_estimate=pl.CostEstimate(flops=10**10, bytes_accessed=0, transcendentals=0),
    )(weight, labels.reshape(1, -1))
    sent = pl.pallas_call(
        forward_kernel,
        in_specs=[far, far, far, vmem, vmem, far],
        out_specs=vmem,
        out_shape=shape((4, 8, 48, TILE), BF16),
        scratch_shapes=[pltpu.VMEM((9, 32, TILE), F32), *scratch],
        compiler_params=tile_params,
    )(tile_count, tile_rows, tile_cols, source, extra, tile_values)
    got = lax.all_to_all(sent.reshape(32, 48, TILE), ("zl", "y", "core"), 0, 0, tiled=True)
    back = pl.pallas_call(
        middle_kernel,
        in_specs=[vmem],
        out_specs=vmem,
        out_shape=shape((8, 80, TILE), BF16),
        scratch_shapes=[pltpu.VMEM((256, TILE), BF16)] * 3,
        compiler_params=params,
    )(got)
    grads = lax.all_to_all(back, DEPTH, 0, 0, tiled=True)
    parts = pl.pallas_call(
        backward_kernel,
        in_specs=[far, far, far, vmem, far],
        out_specs=vmem,
        out_shape=shape((4, 152, 256), BF16),
        scratch_shapes=[pltpu.VMEM((33, 32, TILE), F32), *scratch],
        compiler_params=tile_params,
    )(tile_count, tile_rows, tile_cols, grads, tile_values)
    lines = lax.all_to_all(parts, "x", 0, 0, tiled=True)
    summed = pl.pallas_call(
        sum_kernel,
        in_specs=[vmem],
        out_specs=vmem,
        out_shape=shape((4, 56, 256), BF16),
        compiler_params=params,
    )(lines)
    ours = lax.all_to_all(summed, "zh", 0, 0, tiled=True)
    return pl.pallas_call(
        final_kernel,
        in_specs=[vmem],
        out_specs=(vmem, vmem),
        out_shape=(shape((32, 172), F32), shape((32, 256), F32)),
        compiler_params=params,
    )(ours)


def solution(mesh):
    fine = Mesh(mesh.devices.reshape(4, 4, 4, 4, 2), AXES)
    tiled = ("x", "zh", "zl")
    return jax.shard_map(
        body,
        mesh=fine,
        in_specs=(
            P(DEPTH, ("zl", "x", "zh")),
            P(DEPTH, None),
            P(tiled, None, None),
            P(tiled),
            P(tiled),
            P(tiled),
            P(tiled),
        ),
        out_specs=(P(DEPTH, None), P(DEPTH, ("zl", "x", "zh"))),
        check_vma=False,
    )
```

```python
import jax
import jax.numpy as jnp
from jax import lax
from jax.experimental import pallas as pl
from jax.experimental.pallas import tpu as pltpu
from jax.sharding import Mesh
from jax.sharding import PartitionSpec as P

TILE = 128
STEP = 32
AXES = ("x", "zh", "zl", "y", "core")
DEPTH = ("y", "core")
SMEM = pltpu.MemorySpace.SMEM
F32 = jnp.float32
BF16 = jnp.bfloat16
NT = (((1,), (1,)), ((), ()))
TN = (((0,), (0,)), ((), ()))


def prepare_kernel(near_ref, weight_ref, spread_ref, out_ref):
    for x in range(4):
        spread_ref[x] = near_ref[...]
    weight = weight_ref[...].astype(F32)
    hidden, classes = weight.shape
    rest = jnp.concatenate([weight[:, TILE:], jnp.zeros((hidden, 2 * TILE - classes), F32)], axis=1)
    out_ref[...] = jnp.zeros_like(out_ref)
    out_ref[0:hidden, :] = weight[:, :TILE].astype(BF16)
    out_ref[hidden : 2 * hidden, :] = rest.astype(BF16)


def fetch(pairs, sems):
    copies = [pltpu.make_async_copy(src, dst, sems.at[i]) for i, (src, dst) in enumerate(pairs)]
    for copy in copies:
        copy.start()
    return copies


def tile_copy(tiles_ref, held, sems, step):
    part = pl.ds(step * STEP, STEP)
    return pltpu.make_async_copy(tiles_ref.at[part], held.at[part], sems.at[step])


def forward_kernel(
    count_ref, rows_ref, cols_ref, source_ref, tiles_ref, out_ref, total, count, rows, cols, sems, held, tile_sems
):
    steps = held.shape[0] // STEP
    blocks = total.shape[0] - 1
    small = fetch([(count_ref, count), (rows_ref, rows), (cols_ref, cols)], sems)
    for step in range(steps):
        tile_copy(tiles_ref, held, tile_sems, step).start()
    total[...] = jnp.zeros_like(total)
    for copy in small:
        copy.wait()
    live = count[0]

    @pl.loop(0, steps)
    def work(step):
        tile_copy(tiles_ref, held, tile_sems, step).wait()
        products = []
        for j in range(STEP):
            col = cols[step * STEP + j]
            lanes = pl.ds(pl.multiple_of((col % 2) * TILE, TILE), TILE)
            products.append(
                lax.dot_general(
                    source_ref[col // 2, :, lanes], held[step * STEP + j], NT, preferred_element_type=F32
                )
            )
        for j in range(STEP):
            slot = step * STEP + j
            row = jnp.where(slot < live, rows[slot], blocks)
            total[row] = total[row] + products[j]

    for p in range(blocks):
        block = total[p].astype(BF16)
        for y in range(4):
            out_ref[p // 2, y, p % 2] = block


def middle_kernel(got_ref, wide_ref, labels_ref, out_ref, agg, weight_a, weight_b, held, sem):
    copy = pltpu.make_async_copy(wide_ref.at[:, 0:64, :], held, sem)
    copy.start()
    y = lax.axis_index("y")
    core = lax.axis_index("core")
    for d in range(8):
        sums = got_ref[d].astype(F32)
        for z in range(1, 4):
            sums = sums + got_ref[8 * z + d].astype(F32)
        agg[32 * d : 32 * d + 32, :] = sums.astype(BF16)
    copy.wait()
    for d in range(8):
        weight_a[32 * d : 32 * d + 32, :] = held[d, 0:32, :]
        weight_b[32 * d : 32 * d + 32, :] = held[d, 32:64, :]
    both = labels_ref[...]
    labels = jnp.where(core == 0, both[:, :TILE], both[:, TILE:])
    nodes = agg[...]
    ids = lax.broadcasted_iota(jnp.int32, (TILE, TILE), 0)
    exp_a = jnp.exp(lax.dot_general(weight_a[...], nodes, TN, preferred_element_type=F32))
    logit_b = lax.dot_general(weight_b[...], nodes, TN, preferred_element_type=F32)
    exp_b = jnp.where(ids < 172 - TILE, jnp.exp(logit_b), 0.0)
    whole = jnp.sum(exp_a, axis=0, keepdims=True) + jnp.sum(exp_b, axis=0, keepdims=True)
    delta_a = (exp_a / whole - jnp.where(ids == labels, 1.0, 0.0)).astype(BF16)
    delta_b = (exp_b / whole - jnp.where(ids + TILE == labels, 1.0, 0.0)).astype(BF16)
    mine = pl.ds(pl.multiple_of(y * 64, 64), 64)
    hidden = jnp.dot(weight_a[mine, :], delta_a, preferred_element_type=F32)
    hidden = hidden + jnp.dot(weight_b[mine, :], delta_b, preferred_element_type=F32)
    grad_a = lax.dot_general(agg[mine, :], delta_a, NT, preferred_element_type=F32)
    grad_b = lax.dot_general(agg[mine, :], delta_b, NT, preferred_element_type=F32)
    for c in range(2):
        part = grad_b[32 * c : 32 * c + 32, :64]
        packed = jnp.concatenate([part[0:16], part[16:32]], axis=1)
        block = jnp.concatenate([hidden[32 * c : 32 * c + 32], grad_a[32 * c : 32 * c + 32], packed], axis=0)
        for z in range(4):
            out_ref[2 * z + c] = block.astype(BF16)


def backward_kernel(
    count_ref, rows_ref, cols_ref, got_ref, tiles_ref, out_ref,
    total, count, rows, cols, sems, held, tile_sems,
):
    steps = held.shape[0] // STEP
    blocks = total.shape[0] - 1
    small = fetch([(count_ref, count), (rows_ref, rows), (cols_ref, cols)], sems)
    for step in range(steps):
        tile_copy(tiles_ref, held, tile_sems, step).start()
    total[...] = jnp.zeros_like(total)
    grad_a = got_ref[0, 32:64, :].astype(F32)
    grad_b = got_ref[0, 64:80, :].astype(F32)
    for d in range(1, 8):
        grad_a = grad_a + got_ref[d, 32:64, :].astype(F32)
        grad_b = grad_b + got_ref[d, 64:80, :].astype(F32)
    packed = jnp.concatenate(
        [
            jnp.concatenate([grad_a[0:16], grad_a[16:32]], axis=1),
            jnp.concatenate([grad_b[0:8], grad_b[8:16]], axis=1),
        ],
        axis=0,
    )
    for copy in small:
        copy.wait()
    live = count[0]

    @pl.loop(0, steps)
    def work(step):
        tile_copy(tiles_ref, held, tile_sems, step).wait()
        products = []
        for j in range(STEP):
            row = rows[step * STEP + j]
            products.append(
                jnp.dot(got_ref[row, 0:32, :], held[step * STEP + j], preferred_element_type=F32)
            )
        for j in range(STEP):
            slot = step * STEP + j
            col = jnp.where(slot < live, cols[slot], blocks)
            total[col] = total[col] + products[j]

    for x in range(4):
        blocks_of = [jnp.concatenate([total[2 * p], total[2 * p + 1]], axis=1) for p in range(4 * x, 4 * x + 4)]
        out_ref[x] = jnp.concatenate([*blocks_of, packed], axis=0).astype(BF16)


def sum_kernel(got_ref, out_ref):
    sums = got_ref[0].astype(F32)
    for x in range(1, 4):
        sums = sums + got_ref[x].astype(F32)
    for z in range(4):
        out_ref[z] = jnp.concatenate([sums[32 * z : 32 * z + 32], sums[128:152]], axis=0).astype(BF16)


def final_kernel(got_ref, weight_ref, feature_ref):
    sums = got_ref[0].astype(F32)
    for peer in range(1, 4):
        sums = sums + got_ref[peer].astype(F32)
    feature_ref[...] = sums[0:32]
    grad_a = sums[32:48]
    grad_b = sums[48:56]
    weight_ref[0:16, 0:TILE] = grad_a[:, 0:TILE]
    weight_ref[16:32, 0:TILE] = grad_a[:, TILE:]
    for part in range(2):
        rows = grad_b[:, part * TILE : part * TILE + TILE]
        weight_ref[8 * part : 8 * part + 8, TILE:] = rows[:, 0:44]
        weight_ref[16 + 8 * part : 24 + 8 * part, TILE:] = rows[:, 64:108]


def body(features, weight, tile_values, tile_rows, tile_cols, tile_count, labels):
    shape = jax.ShapeDtypeStruct
    vmem = pl.BlockSpec(memory_space=pltpu.VMEM)
    far = pl.BlockSpec(memory_space=pltpu.MemorySpace.HBM)
    slots = tile_values.shape[0]
    scratch = [
        pltpu.SMEM((1,), jnp.int32),
        pltpu.SMEM((slots,), jnp.int32),
        pltpu.SMEM((slots,), jnp.int32),
        pltpu.SemaphoreType.DMA((3,)),
        pltpu.VMEM(tile_values.shape, BF16),
        pltpu.SemaphoreType.DMA((slots // STEP,)),
    ]
    middle_params = pltpu.CompilerParams(vmem_limit_bytes=213 * 2**18)
    tile_params = pltpu.CompilerParams(vmem_limit_bytes=51 * 2**20)
    params = pltpu.CompilerParams(vmem_limit_bytes=16 * 2**20)
    near = lax.all_gather(features, "zh", axis=0)
    spread, padded = pl.pallas_call(
        prepare_kernel,
        in_specs=[vmem, vmem],
        out_specs=(vmem, vmem),
        out_shape=(shape((4, *near.shape), BF16), shape((512, TILE), BF16)),
        compiler_params=params,
        cost_estimate=pl.CostEstimate(flops=10**10, bytes_accessed=0, transcendentals=0),
    )(near, weight)
    wide = lax.all_gather(padded, DEPTH, axis=0)
    source = lax.all_to_all(spread, "x", 0, 0, tiled=True).reshape(16, *features.shape)
    sent = pl.pallas_call(
        forward_kernel,
        in_specs=[far, far, far, vmem, far],
        out_specs=vmem,
        out_shape=shape((4, 4, 2, 32, TILE), BF16),
        scratch_shapes=[pltpu.VMEM((9, 32, TILE), F32), *scratch],
        compiler_params=tile_params,
    )(tile_count, tile_rows, tile_cols, source, tile_values)
    got = lax.all_to_all(sent.reshape(32, 32, TILE), ("zl", "y", "core"), 0, 0, tiled=True)
    back = pl.pallas_call(
        middle_kernel,
        in_specs=[vmem, far, vmem],
        out_specs=vmem,
        out_shape=shape((8, 80, TILE), BF16),
        scratch_shapes=[pltpu.VMEM((256, TILE), BF16)] * 3
        + [pltpu.VMEM((8, 64, TILE), BF16), pltpu.SemaphoreType.DMA],
        compiler_params=middle_params,
    )(got, wide, labels.reshape(1, -1))
    grads = lax.all_to_all(back, ("zl", "core"), 0, 0, tiled=True)
    parts = pl.pallas_call(
        backward_kernel,
        in_specs=[far, far, far, vmem, far],
        out_specs=vmem,
        out_shape=shape((4, 152, 256), BF16),
        scratch_shapes=[pltpu.VMEM((33, 32, TILE), F32), *scratch],
        compiler_params=tile_params,
    )(tile_count, tile_rows, tile_cols, grads, tile_values)
    lines = lax.all_to_all(parts, "x", 0, 0, tiled=True)
    summed = pl.pallas_call(
        sum_kernel,
        in_specs=[vmem],
        out_specs=vmem,
        out_shape=shape((4, 56, 256), BF16),
        compiler_params=params,
    )(lines)
    ours = lax.all_to_all(summed, "zh", 0, 0, tiled=True)
    return pl.pallas_call(
        final_kernel,
        in_specs=[vmem],
        out_specs=(vmem, vmem),
        out_shape=(shape((32, 172), F32), shape((32, 256), F32)),
        compiler_params=params,
    )(ours)


def solution(mesh):
    fine = Mesh(mesh.devices.reshape(4, 4, 4, 4, 2), AXES)
    tiled = ("x", "zh", "zl")
    return jax.shard_map(
        body,
        mesh=fine,
        in_specs=(
            P(DEPTH, ("zl", "x", "zh")),
            P(DEPTH, None),
            P(tiled, None, None),
            P(tiled),
            P(tiled),
            P(tiled),
            P(tiled),
        ),
        out_specs=(P(DEPTH, None), P(DEPTH, ("zl", "x", "zh"))),
        check_vma=False,
    )
```

```python
import jax
import jax.numpy as jnp
from jax import lax
from jax.experimental import pallas as pl
from jax.experimental.pallas import tpu as pltpu
from jax.sharding import Mesh
from jax.sharding import PartitionSpec as P

TILE = 128
STEP = 64
AXES = ("x", "zh", "zl", "y", "core")
DEPTH = ("y", "core")
F32 = jnp.float32
BF16 = jnp.bfloat16
NT = (((1,), (1,)), ((), ()))
TN = (((0,), (0,)), ((), ()))


def prepare_kernel(
    count_ref, weight_ref, labels_ref, rows_ref, cols_ref, out_ref, row_to_ref, col_to_ref
):
    live = lax.broadcasted_iota(jnp.int32, rows_ref.shape, 1) < count_ref[0]
    row_to_ref[...] = jnp.where(live, rows_ref[...], 8)
    col_to_ref[...] = jnp.where(live, cols_ref[...], 32)
    me = lax.axis_index("zl")
    weight = weight_ref[...].astype(F32)
    classes = weight.shape[1]
    mine = weight[0:8]
    for z in range(1, 4):
        mine = jnp.where(me == z, weight[8 * z : 8 * z + 8], mine)
    labels = labels_ref[...].astype(F32)
    rest = jnp.concatenate([mine[:, TILE:], jnp.zeros((8, 64 - (classes - TILE)), F32)], axis=1)
    for d in range(2):
        half = labels[:, d * TILE : d * TILE + TILE]
        both = jnp.concatenate([half[:, :64], half[:, 64:], jnp.zeros((6, 64), F32)], axis=0)
        right = jnp.concatenate([rest, both], axis=1)
        out_ref[d] = jnp.concatenate([mine[:, :TILE], right], axis=0).astype(BF16)


def spread_kernel(near_ref, extra_ref, out_ref):
    for x in range(4):
        out_ref[x] = near_ref[...]


def scalars(pick_ref, put_ref, pick, put, sems):
    copies = [pltpu.make_async_copy(pick_ref, pick, sems.at[0]), pltpu.make_async_copy(put_ref, put, sems.at[1])]
    for copy in copies:
        copy.start()
    return copies


def forward_kernel(cols_ref, row_to_ref, source_ref, extra_ref, tiles_ref, out_ref, total, cols, row_to, sems):
    steps = tiles_ref.shape[0] // STEP
    blocks = total.shape[0] - 1
    small = scalars(cols_ref, row_to_ref, cols, row_to, sems)
    total[...] = jnp.zeros_like(total)
    for copy in small:
        copy.wait()

    @pl.loop(0, steps)
    def work(step):
        products = []
        for j in range(STEP):
            col = cols[0, step * STEP + j]
            lanes = pl.ds(pl.multiple_of((col % 2) * TILE, TILE), TILE)
            products.append(
                lax.dot_general(
                    source_ref[col // 2, :, lanes], tiles_ref[step * STEP + j], NT, preferred_element_type=F32
                )
            )
        for j in range(STEP):
            row = row_to[0, step * STEP + j]
            total[row] = total[row] + products[j]

    for d in range(blocks):
        block = jnp.concatenate([total[d].astype(BF16), extra_ref[d % 2]], axis=0)
        for z in range(4):
            out_ref[z, d] = block


def middle_kernel(got_ref, out_ref, agg, weight_a, weight_b):
    me = lax.axis_index(DEPTH)
    for d in range(8):
        sums = got_ref[d, 0:32, :].astype(F32)
        for z in range(1, 4):
            sums = sums + got_ref[8 * z + d, 0:32, :].astype(F32)
        agg[32 * d : 32 * d + 32, :] = sums.astype(BF16)
        pieces = [got_ref[8 * z + d, 32:48, :].astype(F32) for z in range(4)]
        weight_a[32 * d : 32 * d + 32, :] = jnp.concatenate([p[0:8] for p in pieces], axis=0).astype(BF16)
        weight_b[32 * d : 32 * d + 32, :] = jnp.concatenate([p[8:16] for p in pieces], axis=0).astype(BF16)
    carrier = got_ref[(me // 2) * 8, 32:48, :].astype(F32)
    labels = jnp.concatenate([carrier[8:9, 64:], carrier[9:10, 64:]], axis=1)
    nodes = agg[...]
    wa = weight_a[...]
    wb = weight_b[...]
    ids = lax.broadcasted_iota(jnp.int32, (TILE, TILE), 0).astype(F32)
    exp_a = jnp.exp(lax.dot_general(wa, nodes, TN, preferred_element_type=F32))
    logit_b = lax.dot_general(wb, nodes, TN, preferred_element_type=F32)
    valid = ids < 172 - TILE
    exp_b = jnp.where(valid, jnp.exp(jnp.where(valid, logit_b, 0.0)), 0.0)
    whole = jnp.sum(exp_a, axis=0, keepdims=True) + jnp.sum(exp_b, axis=0, keepdims=True)
    delta_a = (exp_a / whole - jnp.where(ids == labels, 1.0, 0.0)).astype(BF16)
    delta_b = (exp_b / whole - jnp.where(ids + TILE == labels, 1.0, 0.0)).astype(BF16)
    hidden = jnp.dot(wa, delta_a, preferred_element_type=F32) + jnp.dot(wb, delta_b, preferred_element_type=F32)
    grad_a = lax.dot_general(nodes, delta_a, NT, preferred_element_type=F32)
    grad_b = lax.dot_general(nodes, delta_b, NT, preferred_element_type=F32)
    for d in range(8):
        out_ref[d, 0:32, :] = hidden[32 * d : 32 * d + 32].astype(BF16)
        out_ref[d, 32:64, :] = grad_a[32 * d : 32 * d + 32].astype(BF16)
        part = grad_b[32 * d : 32 * d + 32, :64]
        out_ref[d, 64:80, :] = jnp.concatenate([part[0:16], part[16:32]], axis=1).astype(BF16)


def backward_kernel(rows_ref, col_to_ref, got_ref, tiles_ref, out_ref, total, rows, col_to, sems):
    steps = tiles_ref.shape[0] // STEP
    small = scalars(rows_ref, col_to_ref, rows, col_to, sems)
    total[...] = jnp.zeros_like(total)
    grad_a = got_ref[0, 32:64, :].astype(F32)
    grad_b = got_ref[0, 64:80, :].astype(F32)
    for d in range(1, 8):
        grad_a = grad_a + got_ref[d, 32:64, :].astype(F32)
        grad_b = grad_b + got_ref[d, 64:80, :].astype(F32)
    packed = jnp.concatenate(
        [
            jnp.concatenate([grad_a[0:16], grad_a[16:32]], axis=1),
            jnp.concatenate([grad_b[0:8], grad_b[8:16]], axis=1),
        ],
        axis=0,
    )
    for copy in small:
        copy.wait()

    @pl.loop(0, steps)
    def work(step):
        products = []
        for j in range(STEP):
            row = rows[0, step * STEP + j]
            products.append(
                jnp.dot(got_ref[row, 0:32, :], tiles_ref[step * STEP + j], preferred_element_type=F32)
            )
        for j in range(STEP):
            col = col_to[0, step * STEP + j]
            total[col] = total[col] + products[j]

    for x in range(4):
        blocks_of = [jnp.concatenate([total[2 * p], total[2 * p + 1]], axis=1) for p in range(4 * x, 4 * x + 4)]
        out_ref[x] = jnp.concatenate([*blocks_of, packed], axis=0).astype(BF16)


def sum_kernel(got_ref, out_ref):
    sums = got_ref[0].astype(F32)
    for x in range(1, 4):
        sums = sums + got_ref[x].astype(F32)
    for z in range(4):
        out_ref[z] = jnp.concatenate([sums[32 * z : 32 * z + 32], sums[128:152]], axis=0).astype(BF16)


def final_kernel(got_ref, weight_ref, feature_ref):
    sums = got_ref[0].astype(F32)
    for peer in range(1, 4):
        sums = sums + got_ref[peer].astype(F32)
    feature_ref[...] = sums[0:32]
    grad_a = sums[32:48]
    grad_b = sums[48:56]
    weight_ref[0:16, 0:TILE] = grad_a[:, 0:TILE]
    weight_ref[16:32, 0:TILE] = grad_a[:, TILE:]
    for part in range(2):
        rows = grad_b[:, part * TILE : part * TILE + TILE]
        weight_ref[8 * part : 8 * part + 8, TILE:] = rows[:, 0:44]
        weight_ref[16 + 8 * part : 24 + 8 * part, TILE:] = rows[:, 64:108]


def body(features, weight, tile_values, tile_rows, tile_cols, tile_count, labels):
    shape = jax.ShapeDtypeStruct
    vmem = pl.BlockSpec(memory_space=pltpu.VMEM)
    far = pl.BlockSpec(memory_space=pltpu.MemorySpace.HBM)
    slots = tile_values.shape[0]
    scratch = [
        pltpu.SMEM((1, slots), jnp.int32),
        pltpu.SMEM((1, slots), jnp.int32),
        pltpu.SemaphoreType.DMA((2,)),
    ]
    params = pltpu.CompilerParams(vmem_limit_bytes=16 * 2**20)
    near = lax.all_to_all(jnp.broadcast_to(features[None], (4, *features.shape)), "zh", 0, 0, tiled=True)
    rows = tile_rows.reshape(1, slots)
    cols = tile_cols.reshape(1, slots)
    extra, row_to, col_to = pl.pallas_call(
        prepare_kernel,
        in_specs=[pl.BlockSpec(memory_space=pltpu.MemorySpace.SMEM)] + [vmem] * 4,
        out_specs=(vmem,) * 3,
        out_shape=(shape((2, 16, TILE), BF16), shape(rows.shape, jnp.int32), shape(cols.shape, jnp.int32)),
        compiler_params=params,
        cost_estimate=pl.CostEstimate(flops=10**10, bytes_accessed=0, transcendentals=0),
    )(tile_count, weight, labels.reshape(1, -1), rows, cols)
    spread = pl.pallas_call(
        spread_kernel,
        in_specs=[vmem, far],
        out_specs=vmem,
        out_shape=shape((4, *near.shape), BF16),
        compiler_params=params,
        cost_estimate=pl.CostEstimate(flops=10**10, bytes_accessed=0, transcendentals=0),
    )(near, extra)
    source = lax.all_to_all(spread, "x", 0, 0, tiled=True).reshape(16, *features.shape)
    sent = pl.pallas_call(
        forward_kernel,
        in_specs=[far, far, vmem, vmem, vmem],
        out_specs=vmem,
        out_shape=shape((4, 8, 48, TILE), BF16),
        scratch_shapes=[pltpu.VMEM((9, 32, TILE), F32), *scratch],
        compiler_params=params,
    )(cols, row_to, source, extra, tile_values)
    got = lax.all_to_all(sent.reshape(32, 48, TILE), ("zl", "y", "core"), 0, 0, tiled=True)
    back = pl.pallas_call(
        middle_kernel,
        in_specs=[vmem],
        out_specs=vmem,
        out_shape=shape((8, 80, TILE), BF16),
        scratch_shapes=[pltpu.VMEM((256, TILE), BF16)] * 3,
        compiler_params=params,
        cost_estimate=pl.CostEstimate(flops=10**10, bytes_accessed=0, transcendentals=0),
    )(got)
    grads = lax.all_to_all(back, DEPTH, 0, 0, tiled=True)
    parts = pl.pallas_call(
        backward_kernel,
        in_specs=[far, far, vmem, vmem],
        out_specs=vmem,
        out_shape=shape((4, 152, 256), BF16),
        scratch_shapes=[pltpu.VMEM((33, 32, TILE), F32), *scratch],
        compiler_params=params,
    )(rows, col_to, grads, tile_values)
    lines = lax.all_to_all(parts, "x", 0, 0, tiled=True)
    summed = pl.pallas_call(
        sum_kernel,
        in_specs=[vmem],
        out_specs=vmem,
        out_shape=shape((4, 56, 256), BF16),
        compiler_params=params,
    )(lines)
    ours = lax.all_to_all(summed, "zh", 0, 0, tiled=True)
    return pl.pallas_call(
        final_kernel,
        in_specs=[vmem],
        out_specs=(vmem, vmem),
        out_shape=(shape((32, 172), F32), shape((32, 256), F32)),
        compiler_params=params,
    )(ours)


def solution(mesh):
    fine = Mesh(mesh.devices.reshape(4, 4, 4, 4, 2), AXES)
    tiled = ("x", "zh", "zl")
    return jax.shard_map(
        body,
        mesh=fine,
        in_specs=(
            P(DEPTH, ("zl", "x", "zh")),
            P(DEPTH, None),
            P(tiled, None, None),
            P(tiled),
            P(tiled),
            P(tiled),
            P(tiled),
        ),
        out_specs=(P(DEPTH, None), P(DEPTH, ("zl", "x", "zh"))),
        check_vma=False,
    )
```

```python
import jax
import jax.numpy as jnp
from jax import lax
from jax.experimental import pallas as pl
from jax.experimental.pallas import tpu as pltpu
from jax.sharding import Mesh
from jax.sharding import PartitionSpec as P

TILE = 128
STEP = 64
AXES = ("x", "zh", "zl", "y", "core")
DEPTH = ("y", "core")
F32 = jnp.float32
BF16 = jnp.bfloat16
NT = (((1,), (1,)), ((), ()))
TN = (((0,), (0,)), ((), ()))


def spread_kernel(count_ref, near_ref, out_ref, count_out_ref):
    for x in range(4):
        out_ref[x] = near_ref[...]
    count_out_ref[...] = jnp.full(count_out_ref.shape, count_ref[0], jnp.int32)


def scalars(refs, held, sems):
    copies = [pltpu.make_async_copy(src, dst, sems.at[i]) for i, (src, dst) in enumerate(zip(refs, held))]
    for copy in copies:
        copy.start()
    return copies


def packed_rows(weight_ref, labels_ref, half):
    me = lax.axis_index("zl")
    weight = weight_ref[...].astype(F32)
    classes = weight.shape[1]
    mine = weight[0:8]
    for z in range(1, 4):
        mine = jnp.where(me == z, weight[8 * z : 8 * z + 8], mine)
    labels = labels_ref[:, half * TILE : half * TILE + TILE].astype(F32)
    rest = jnp.concatenate([mine[:, TILE:], jnp.zeros((8, 64 - (classes - TILE)), F32)], axis=1)
    both = jnp.concatenate([labels[:, :64], labels[:, 64:], jnp.zeros((6, 64), F32)], axis=0)
    return jnp.concatenate([mine[:, :TILE], jnp.concatenate([rest, both], axis=1)], axis=0).astype(BF16)


def forward_kernel(
    count_ref, rows_ref, cols_ref, source_ref, weight_ref, labels_ref, tiles_ref, out_ref,
    total, count, rows, cols, sems,
):
    steps = tiles_ref.shape[0] // STEP
    blocks = total.shape[0] - 1
    small = scalars((count_ref, rows_ref, cols_ref), (count, rows, cols), sems)
    total[...] = jnp.zeros_like(total)
    extra = [packed_rows(weight_ref, labels_ref, half) for half in range(2)]
    for copy in small:
        copy.wait()
    live = count[0, 0]

    @pl.loop(0, steps)
    def work(step):
        products = []
        for j in range(STEP):
            col = cols[0, step * STEP + j]
            lanes = pl.ds(pl.multiple_of((col % 2) * TILE, TILE), TILE)
            products.append(
                lax.dot_general(
                    source_ref[col // 2, :, lanes], tiles_ref[step * STEP + j], NT, preferred_element_type=F32
                )
            )
        for j in range(STEP):
            slot = step * STEP + j
            row = jnp.where(slot < live, rows[0, slot], blocks)
            total[row] = total[row] + products[j]

    for d in range(blocks):
        block = jnp.concatenate([total[d].astype(BF16), extra[d % 2]], axis=0)
        for z in range(4):
            out_ref[z, d] = block


def middle_kernel(got_ref, out_ref, agg, weight_a, weight_b):
    me = lax.axis_index(DEPTH)
    for d in range(8):
        sums = got_ref[d, 0:32, :].astype(F32)
        for z in range(1, 4):
            sums = sums + got_ref[8 * z + d, 0:32, :].astype(F32)
        agg[32 * d : 32 * d + 32, :] = sums.astype(BF16)
        pieces = [got_ref[8 * z + d, 32:48, :].astype(F32) for z in range(4)]
        weight_a[32 * d : 32 * d + 32, :] = jnp.concatenate([p[0:8] for p in pieces], axis=0).astype(BF16)
        weight_b[32 * d : 32 * d + 32, :] = jnp.concatenate([p[8:16] for p in pieces], axis=0).astype(BF16)
    carrier = got_ref[(me // 2) * 8, 32:48, :].astype(F32)
    labels = jnp.concatenate([carrier[8:9, 64:], carrier[9:10, 64:]], axis=1)
    nodes = agg[...]
    wa = weight_a[...]
    wb = weight_b[...]
    ids = lax.broadcasted_iota(jnp.int32, (TILE, TILE), 0).astype(F32)
    exp_a = jnp.exp(lax.dot_general(wa, nodes, TN, preferred_element_type=F32))
    logit_b = lax.dot_general(wb, nodes, TN, preferred_element_type=F32)
    valid = ids < 172 - TILE
    exp_b = jnp.where(valid, jnp.exp(jnp.where(valid, logit_b, 0.0)), 0.0)
    whole = jnp.sum(exp_a, axis=0, keepdims=True) + jnp.sum(exp_b, axis=0, keepdims=True)
    delta_a = (exp_a / whole - jnp.where(ids == labels, 1.0, 0.0)).astype(BF16)
    delta_b = (exp_b / whole - jnp.where(ids + TILE == labels, 1.0, 0.0)).astype(BF16)
    hidden = jnp.dot(wa, delta_a, preferred_element_type=F32) + jnp.dot(wb, delta_b, preferred_element_type=F32)
    grad_a = lax.dot_general(nodes, delta_a, NT, preferred_element_type=F32)
    grad_b = lax.dot_general(nodes, delta_b, NT, preferred_element_type=F32)
    for d in range(8):
        out_ref[d, 0:32, :] = hidden[32 * d : 32 * d + 32].astype(BF16)
        out_ref[d, 32:64, :] = grad_a[32 * d : 32 * d + 32].astype(BF16)
        part = grad_b[32 * d : 32 * d + 32, :64]
        out_ref[d, 64:80, :] = jnp.concatenate([part[0:16], part[16:32]], axis=1).astype(BF16)


def backward_kernel(
    count_ref, rows_ref, cols_ref, got_ref, tiles_ref, out_ref, total, count, rows, cols, sems
):
    steps = tiles_ref.shape[0] // STEP
    blocks = total.shape[0] - 1
    small = scalars((count_ref, rows_ref, cols_ref), (count, rows, cols), sems)
    total[...] = jnp.zeros_like(total)
    grad_a = got_ref[0, 32:64, :].astype(F32)
    grad_b = got_ref[0, 64:80, :].astype(F32)
    for d in range(1, 8):
        grad_a = grad_a + got_ref[d, 32:64, :].astype(F32)
        grad_b = grad_b + got_ref[d, 64:80, :].astype(F32)
    packed = jnp.concatenate(
        [
            jnp.concatenate([grad_a[0:16], grad_a[16:32]], axis=1),
            jnp.concatenate([grad_b[0:8], grad_b[8:16]], axis=1),
        ],
        axis=0,
    )
    for copy in small:
        copy.wait()

    live = count[0, 0]

    @pl.loop(0, steps)
    def work(step):
        products = []
        for j in range(STEP):
            row = rows[0, step * STEP + j]
            products.append(
                jnp.dot(got_ref[row, 0:32, :], tiles_ref[step * STEP + j], preferred_element_type=F32)
            )
        for j in range(STEP):
            slot = step * STEP + j
            col = jnp.where(slot < live, cols[0, slot], blocks)
            total[col] = total[col] + products[j]

    for x in range(4):
        blocks_of = [jnp.concatenate([total[2 * p], total[2 * p + 1]], axis=1) for p in range(4 * x, 4 * x + 4)]
        out_ref[x] = jnp.concatenate([*blocks_of, packed], axis=0).astype(BF16)


def sum_kernel(got_ref, out_ref):
    sums = got_ref[0].astype(F32)
    for x in range(1, 4):
        sums = sums + got_ref[x].astype(F32)
    for z in range(4):
        out_ref[z] = jnp.concatenate([sums[32 * z : 32 * z + 32], sums[128:152]], axis=0).astype(BF16)


def final_kernel(got_ref, weight_ref, feature_ref):
    sums = got_ref[0].astype(F32)
    for peer in range(1, 4):
        sums = sums + got_ref[peer].astype(F32)
    feature_ref[...] = sums[0:32]
    grad_a = sums[32:48]
    grad_b = sums[48:56]
    weight_ref[0:16, 0:TILE] = grad_a[:, 0:TILE]
    weight_ref[16:32, 0:TILE] = grad_a[:, TILE:]
    for part in range(2):
        rows = grad_b[:, part * TILE : part * TILE + TILE]
        weight_ref[8 * part : 8 * part + 8, TILE:] = rows[:, 0:44]
        weight_ref[16 + 8 * part : 24 + 8 * part, TILE:] = rows[:, 64:108]


def body(features, weight, tile_values, tile_rows, tile_cols, tile_count, labels):
    shape = jax.ShapeDtypeStruct
    vmem = pl.BlockSpec(memory_space=pltpu.VMEM)
    far = pl.BlockSpec(memory_space=pltpu.MemorySpace.HBM)
    slots = tile_values.shape[0]
    scratch = [
        pltpu.SMEM((1, TILE), jnp.int32),
        pltpu.SMEM((1, slots), jnp.int32),
        pltpu.SMEM((1, slots), jnp.int32),
        pltpu.SemaphoreType.DMA((3,)),
    ]
    params = pltpu.CompilerParams(vmem_limit_bytes=16 * 2**20)
    rows = tile_rows.reshape(1, slots)
    cols = tile_cols.reshape(1, slots)
    near = lax.all_gather(features, "zh", axis=0)
    spread, count = pl.pallas_call(
        spread_kernel,
        in_specs=[pl.BlockSpec(memory_space=pltpu.MemorySpace.SMEM), vmem],
        out_specs=(vmem, vmem),
        out_shape=(shape((4, *near.shape), BF16), shape((1, TILE), jnp.int32)),
        compiler_params=params,
        cost_estimate=pl.CostEstimate(flops=10**10, bytes_accessed=0, transcendentals=0),
    )(tile_count, near)
    source = lax.all_to_all(spread, "x", 0, 0, tiled=True).reshape(16, *features.shape)
    sent = pl.pallas_call(
        forward_kernel,
        in_specs=[far, far, far, vmem, vmem, vmem, vmem],
        out_specs=vmem,
        out_shape=shape((4, 8, 48, TILE), BF16),
        scratch_shapes=[pltpu.VMEM((9, 32, TILE), F32), *scratch],
        compiler_params=params,
    )(count, rows, cols, source, weight, labels.reshape(1, -1), tile_values)
    got = lax.all_to_all(sent.reshape(32, 48, TILE), ("zl", "y", "core"), 0, 0, tiled=True)
    back = pl.pallas_call(
        middle_kernel,
        in_specs=[vmem],
        out_specs=vmem,
        out_shape=shape((8, 80, TILE), BF16),
        scratch_shapes=[pltpu.VMEM((256, TILE), BF16)] * 3,
        compiler_params=params,
        cost_estimate=pl.CostEstimate(flops=10**10, bytes_accessed=0, transcendentals=0),
    )(got)
    grads = lax.all_to_all(back, DEPTH, 0, 0, tiled=True)
    parts = pl.pallas_call(
        backward_kernel,
        in_specs=[far, far, far, vmem, vmem],
        out_specs=vmem,
        out_shape=shape((4, 152, 256), BF16),
        scratch_shapes=[pltpu.VMEM((33, 32, TILE), F32), *scratch],
        compiler_params=params,
    )(count, rows, cols, grads, tile_values)
    lines = lax.all_to_all(parts, "x", 0, 0, tiled=True)
    summed = pl.pallas_call(
        sum_kernel,
        in_specs=[vmem],
        out_specs=vmem,
        out_shape=shape((4, 56, 256), BF16),
        compiler_params=params,
    )(lines)
    ours = lax.all_to_all(summed, "zh", 0, 0, tiled=True)
    return pl.pallas_call(
        final_kernel,
        in_specs=[vmem],
        out_specs=(vmem, vmem),
        out_shape=(shape((32, 172), F32), shape((32, 256), F32)),
        compiler_params=params,
    )(ours)


def solution(mesh):
    fine = Mesh(mesh.devices.reshape(4, 4, 4, 4, 2), AXES)
    tiled = ("x", "zh", "zl")
    return jax.shard_map(
        body,
        mesh=fine,
        in_specs=(
            P(DEPTH, ("zl", "x", "zh")),
            P(DEPTH, None),
            P(tiled, None, None),
            P(tiled),
            P(tiled),
            P(tiled),
            P(tiled),
        ),
        out_specs=(P(DEPTH, None), P(DEPTH, ("zl", "x", "zh"))),
        check_vma=False,
    )
```

```python
import jax
import jax.numpy as jnp
from jax import lax
from jax.experimental import pallas as pl
from jax.experimental.pallas import tpu as pltpu
from jax.sharding import Mesh
from jax.sharding import PartitionSpec as P

TILE = 128
STEP = 64
AXES = ("x", "zh", "zl", "y", "core")
DEPTH = ("y", "core")
F32 = jnp.float32
BF16 = jnp.bfloat16
NT = (((1,), (1,)), ((), ()))
TN = (((0,), (0,)), ((), ()))


def spread_kernel(count_ref, near_ref, out_ref, count_out_ref):
    for x in range(4):
        out_ref[x] = near_ref[...]
    count_out_ref[...] = jnp.full(count_out_ref.shape, count_ref[0], jnp.int32)


def scalars(refs, held, sems):
    copies = [pltpu.make_async_copy(src, dst, sems.at[i]) for i, (src, dst) in enumerate(zip(refs, held))]
    for copy in copies:
        copy.start()
    return copies


def packed_rows(weight_ref, labels_ref, half):
    me = lax.axis_index("zl")
    weight = weight_ref[...].astype(F32)
    classes = weight.shape[1]
    mine = weight[0:8]
    for z in range(1, 4):
        mine = jnp.where(me == z, weight[8 * z : 8 * z + 8], mine)
    labels = labels_ref[:, half * TILE : half * TILE + TILE].astype(F32)
    rest = jnp.concatenate([mine[:, TILE:], jnp.zeros((8, 64 - (classes - TILE)), F32)], axis=1)
    both = jnp.concatenate([labels[:, :64], labels[:, 64:], jnp.zeros((6, 64), F32)], axis=0)
    return jnp.concatenate([mine[:, :TILE], jnp.concatenate([rest, both], axis=1)], axis=0).astype(BF16)


def forward_kernel(
    count_ref, rows_ref, cols_ref, source_ref, weight_ref, labels_ref, tiles_ref, out_ref,
    total, count, rows, cols, sems,
):
    blocks = total.shape[0] - 1
    small = scalars((count_ref, rows_ref, cols_ref), (count, rows, cols), sems)
    total[...] = jnp.zeros_like(total)
    extra = [packed_rows(weight_ref, labels_ref, half) for half in range(2)]
    for copy in small:
        copy.wait()
    live = count[0, 0]

    @pl.loop(0, (live + STEP - 1) // STEP)
    def work(step):
        products = []
        for j in range(STEP):
            col = cols[0, step * STEP + j]
            lanes = pl.ds(pl.multiple_of((col % 2) * TILE, TILE), TILE)
            products.append(
                lax.dot_general(
                    source_ref[col // 2, :, lanes], tiles_ref[step * STEP + j], NT, preferred_element_type=F32
                )
            )
        for j in range(STEP):
            slot = step * STEP + j
            row = jnp.where(slot < live, rows[0, slot], blocks)
            total[row] = total[row] + products[j]

    for d in range(blocks):
        block = jnp.concatenate([total[d].astype(BF16), extra[d % 2]], axis=0)
        for z in range(4):
            out_ref[z, d] = block


def middle_kernel(got_ref, out_ref, agg, weight_a, weight_b):
    me = lax.axis_index(DEPTH)
    for d in range(8):
        sums = got_ref[d, 0:32, :].astype(F32)
        for z in range(1, 4):
            sums = sums + got_ref[8 * z + d, 0:32, :].astype(F32)
        agg[32 * d : 32 * d + 32, :] = sums.astype(BF16)
        pieces = [got_ref[8 * z + d, 32:48, :].astype(F32) for z in range(4)]
        weight_a[32 * d : 32 * d + 32, :] = jnp.concatenate([p[0:8] for p in pieces], axis=0).astype(BF16)
        weight_b[32 * d : 32 * d + 32, :] = jnp.concatenate([p[8:16] for p in pieces], axis=0).astype(BF16)
    carrier = got_ref[(me // 2) * 8, 32:48, :].astype(F32)
    labels = jnp.concatenate([carrier[8:9, 64:], carrier[9:10, 64:]], axis=1)
    nodes = agg[...]
    wa = weight_a[...]
    wb = weight_b[...]
    ids = lax.broadcasted_iota(jnp.int32, (TILE, TILE), 0).astype(F32)
    exp_a = jnp.exp(lax.dot_general(wa, nodes, TN, preferred_element_type=F32))
    logit_b = lax.dot_general(wb, nodes, TN, preferred_element_type=F32)
    valid = ids < 172 - TILE
    exp_b = jnp.where(valid, jnp.exp(jnp.where(valid, logit_b, 0.0)), 0.0)
    whole = jnp.sum(exp_a, axis=0, keepdims=True) + jnp.sum(exp_b, axis=0, keepdims=True)
    delta_a = (exp_a / whole - jnp.where(ids == labels, 1.0, 0.0)).astype(BF16)
    delta_b = (exp_b / whole - jnp.where(ids + TILE == labels, 1.0, 0.0)).astype(BF16)
    hidden = jnp.dot(wa, delta_a, preferred_element_type=F32) + jnp.dot(wb, delta_b, preferred_element_type=F32)
    grad_a = lax.dot_general(nodes, delta_a, NT, preferred_element_type=F32)
    grad_b = lax.dot_general(nodes, delta_b, NT, preferred_element_type=F32)
    for d in range(8):
        out_ref[d, 0:32, :] = hidden[32 * d : 32 * d + 32].astype(BF16)
        out_ref[d, 32:64, :] = grad_a[32 * d : 32 * d + 32].astype(BF16)
        part = grad_b[32 * d : 32 * d + 32, :64]
        out_ref[d, 64:80, :] = jnp.concatenate([part[0:16], part[16:32]], axis=1).astype(BF16)


def backward_kernel(
    count_ref, rows_ref, cols_ref, got_ref, tiles_ref, out_ref, total, count, rows, cols, sems
):
    blocks = total.shape[0] - 1
    small = scalars((count_ref, rows_ref, cols_ref), (count, rows, cols), sems)
    total[...] = jnp.zeros_like(total)
    grad_a = got_ref[0, 32:64, :].astype(F32)
    grad_b = got_ref[0, 64:80, :].astype(F32)
    for d in range(1, 8):
        grad_a = grad_a + got_ref[d, 32:64, :].astype(F32)
        grad_b = grad_b + got_ref[d, 64:80, :].astype(F32)
    packed = jnp.concatenate(
        [
            jnp.concatenate([grad_a[0:16], grad_a[16:32]], axis=1),
            jnp.concatenate([grad_b[0:8], grad_b[8:16]], axis=1),
        ],
        axis=0,
    )
    for copy in small:
        copy.wait()

    live = count[0, 0]

    @pl.loop(0, (live + STEP - 1) // STEP)
    def work(step):
        products = []
        for j in range(STEP):
            row = rows[0, step * STEP + j]
            products.append(
                jnp.dot(got_ref[row, 0:32, :], tiles_ref[step * STEP + j], preferred_element_type=F32)
            )
        for j in range(STEP):
            slot = step * STEP + j
            col = jnp.where(slot < live, cols[0, slot], blocks)
            total[col] = total[col] + products[j]

    for x in range(4):
        blocks_of = [jnp.concatenate([total[2 * p], total[2 * p + 1]], axis=1) for p in range(4 * x, 4 * x + 4)]
        out_ref[x] = jnp.concatenate([*blocks_of, packed], axis=0).astype(BF16)


def sum_kernel(got_ref, out_ref):
    sums = got_ref[0].astype(F32)
    for x in range(1, 4):
        sums = sums + got_ref[x].astype(F32)
    for z in range(4):
        out_ref[z] = jnp.concatenate([sums[32 * z : 32 * z + 32], sums[128:152]], axis=0).astype(BF16)


def final_kernel(got_ref, weight_ref, feature_ref):
    sums = got_ref[0].astype(F32)
    for peer in range(1, 4):
        sums = sums + got_ref[peer].astype(F32)
    feature_ref[...] = sums[0:32]
    grad_a = sums[32:48]
    grad_b = sums[48:56]
    weight_ref[0:16, 0:TILE] = grad_a[:, 0:TILE]
    weight_ref[16:32, 0:TILE] = grad_a[:, TILE:]
    for part in range(2):
        rows = grad_b[:, part * TILE : part * TILE + TILE]
        weight_ref[8 * part : 8 * part + 8, TILE:] = rows[:, 0:44]
        weight_ref[16 + 8 * part : 24 + 8 * part, TILE:] = rows[:, 64:108]


def body(features, weight, tile_values, tile_rows, tile_cols, tile_count, labels):
    shape = jax.ShapeDtypeStruct
    vmem = pl.BlockSpec(memory_space=pltpu.VMEM)
    far = pl.BlockSpec(memory_space=pltpu.MemorySpace.HBM)
    slots = tile_values.shape[0]
    scratch = [
        pltpu.SMEM((1, TILE), jnp.int32),
        pltpu.SMEM((1, slots), jnp.int32),
        pltpu.SMEM((1, slots), jnp.int32),
        pltpu.SemaphoreType.DMA((3,)),
    ]
    params = pltpu.CompilerParams(vmem_limit_bytes=16 * 2**20)
    rows = tile_rows.reshape(1, slots)
    cols = tile_cols.reshape(1, slots)
    near = lax.all_gather(features, "zh", axis=0)
    spread, count = pl.pallas_call(
        spread_kernel,
        in_specs=[pl.BlockSpec(memory_space=pltpu.MemorySpace.SMEM), vmem],
        out_specs=(vmem, vmem),
        out_shape=(shape((4, *near.shape), BF16), shape((1, TILE), jnp.int32)),
        compiler_params=params,
        cost_estimate=pl.CostEstimate(flops=10**10, bytes_accessed=0, transcendentals=0),
    )(tile_count, near)
    source = lax.all_to_all(spread, "x", 0, 0, tiled=True).reshape(16, *features.shape)
    sent = pl.pallas_call(
        forward_kernel,
        in_specs=[far, far, far, vmem, vmem, vmem, vmem],
        out_specs=vmem,
        out_shape=shape((4, 8, 48, TILE), BF16),
        scratch_shapes=[pltpu.VMEM((9, 32, TILE), F32), *scratch],
        compiler_params=params,
    )(count, rows, cols, source, weight, labels.reshape(1, -1), tile_values)
    got = lax.all_to_all(sent.reshape(32, 48, TILE), ("zl", "y", "core"), 0, 0, tiled=True)
    back = pl.pallas_call(
        middle_kernel,
        in_specs=[vmem],
        out_specs=vmem,
        out_shape=shape((8, 80, TILE), BF16),
        scratch_shapes=[pltpu.VMEM((256, TILE), BF16)] * 3,
        compiler_params=params,
        cost_estimate=pl.CostEstimate(flops=10**10, bytes_accessed=0, transcendentals=0),
    )(got)
    grads = lax.all_to_all(back, DEPTH, 0, 0, tiled=True)
    parts = pl.pallas_call(
        backward_kernel,
        in_specs=[far, far, far, vmem, vmem],
        out_specs=vmem,
        out_shape=shape((4, 152, 256), BF16),
        scratch_shapes=[pltpu.VMEM((33, 32, TILE), F32), *scratch],
        compiler_params=params,
    )(count, rows, cols, grads, tile_values)
    lines = lax.all_to_all(parts, "x", 0, 0, tiled=True)
    summed = pl.pallas_call(
        sum_kernel,
        in_specs=[vmem],
        out_specs=vmem,
        out_shape=shape((4, 56, 256), BF16),
        compiler_params=params,
    )(lines)
    ours = lax.all_to_all(summed, "zh", 0, 0, tiled=True)
    return pl.pallas_call(
        final_kernel,
        in_specs=[vmem],
        out_specs=(vmem, vmem),
        out_shape=(shape((32, 172), F32), shape((32, 256), F32)),
        compiler_params=params,
    )(ours)


def solution(mesh):
    fine = Mesh(mesh.devices.reshape(4, 4, 4, 4, 2), AXES)
    tiled = ("x", "zh", "zl")
    return jax.shard_map(
        body,
        mesh=fine,
        in_specs=(
            P(DEPTH, ("zl", "x", "zh")),
            P(DEPTH, None),
            P(tiled, None, None),
            P(tiled),
            P(tiled),
            P(tiled),
            P(tiled),
        ),
        out_specs=(P(DEPTH, None), P(DEPTH, ("zl", "x", "zh"))),
        check_vma=False,
    )
```

```python
import jax
import jax.numpy as jnp
from jax import lax
from jax.experimental import pallas as pl
from jax.experimental.pallas import tpu as pltpu
from jax.sharding import Mesh
from jax.sharding import PartitionSpec as P

TILE = 128
STEP = 64
AXES = ("x", "zh", "zl", "y", "core")
DEPTH = ("y", "core")
F32 = jnp.float32
BF16 = jnp.bfloat16
NT = (((1,), (1,)), ((), ()))
TN = (((0,), (0,)), ((), ()))


def first_kernel(count_ref, own_ref, out_ref, count_out_ref):
    for z in range(4):
        out_ref[z] = own_ref[...]
    count_out_ref[...] = jnp.full(count_out_ref.shape, count_ref[0], jnp.int32)


def spread_kernel(near_ref, count_ref, out_ref):
    for x in range(4):
        out_ref[x] = near_ref[...]


def scalars(refs, held, sems):
    copies = [pltpu.make_async_copy(src, dst, sems.at[i]) for i, (src, dst) in enumerate(zip(refs, held))]
    for copy in copies:
        copy.start()
    return copies


def packed_rows(weight_ref, labels_ref, half):
    me = lax.axis_index("zl")
    weight = weight_ref[...].astype(F32)
    classes = weight.shape[1]
    mine = weight[0:8]
    for z in range(1, 4):
        mine = jnp.where(me == z, weight[8 * z : 8 * z + 8], mine)
    labels = labels_ref[:, half * TILE : half * TILE + TILE].astype(F32)
    rest = jnp.concatenate([mine[:, TILE:], jnp.zeros((8, 64 - (classes - TILE)), F32)], axis=1)
    both = jnp.concatenate([labels[:, :64], labels[:, 64:], jnp.zeros((6, 64), F32)], axis=0)
    return jnp.concatenate([mine[:, :TILE], jnp.concatenate([rest, both], axis=1)], axis=0).astype(BF16)


def forward_kernel(
    count_ref, rows_ref, cols_ref, source_ref, weight_ref, labels_ref, tiles_ref, out_ref,
    total, count, rows, cols, sems,
):
    blocks = total.shape[0] - 1
    small = scalars((count_ref, rows_ref, cols_ref), (count, rows, cols), sems)
    total[...] = jnp.zeros_like(total)
    extra = [packed_rows(weight_ref, labels_ref, half) for half in range(2)]
    for copy in small:
        copy.wait()
    live = count[0, 0]

    @pl.loop(0, (live + STEP - 1) // STEP)
    def work(step):
        products = []
        for j in range(STEP):
            col = cols[0, step * STEP + j]
            lanes = pl.ds(pl.multiple_of((col % 2) * TILE, TILE), TILE)
            products.append(
                lax.dot_general(
                    source_ref[col // 2, :, lanes], tiles_ref[step * STEP + j], NT, preferred_element_type=F32
                )
            )
        for j in range(STEP):
            slot = step * STEP + j
            row = jnp.where(slot < live, rows[0, slot], blocks)
            total[row] = total[row] + products[j]

    for d in range(blocks):
        block = jnp.concatenate([total[d].astype(BF16), extra[d % 2]], axis=0)
        for z in range(4):
            out_ref[z, d] = block


def middle_kernel(got_ref, out_ref, agg, weight_a, weight_b):
    me = lax.axis_index(DEPTH)
    for d in range(8):
        sums = got_ref[d, 0:32, :].astype(F32)
        for z in range(1, 4):
            sums = sums + got_ref[8 * z + d, 0:32, :].astype(F32)
        agg[32 * d : 32 * d + 32, :] = sums.astype(BF16)
        pieces = [got_ref[8 * z + d, 32:48, :].astype(F32) for z in range(4)]
        weight_a[32 * d : 32 * d + 32, :] = jnp.concatenate([p[0:8] for p in pieces], axis=0).astype(BF16)
        weight_b[32 * d : 32 * d + 32, :] = jnp.concatenate([p[8:16] for p in pieces], axis=0).astype(BF16)
    carrier = got_ref[(me // 2) * 8, 32:48, :].astype(F32)
    labels = jnp.concatenate([carrier[8:9, 64:], carrier[9:10, 64:]], axis=1)
    nodes = agg[...]
    wa = weight_a[...]
    wb = weight_b[...]
    ids = lax.broadcasted_iota(jnp.int32, (TILE, TILE), 0).astype(F32)
    exp_a = jnp.exp(lax.dot_general(wa, nodes, TN, preferred_element_type=F32))
    logit_b = lax.dot_general(wb, nodes, TN, preferred_element_type=F32)
    valid = ids < 172 - TILE
    exp_b = jnp.where(valid, jnp.exp(jnp.where(valid, logit_b, 0.0)), 0.0)
    whole = jnp.sum(exp_a, axis=0, keepdims=True) + jnp.sum(exp_b, axis=0, keepdims=True)
    delta_a = (exp_a / whole - jnp.where(ids == labels, 1.0, 0.0)).astype(BF16)
    delta_b = (exp_b / whole - jnp.where(ids + TILE == labels, 1.0, 0.0)).astype(BF16)
    hidden = jnp.dot(wa, delta_a, preferred_element_type=F32) + jnp.dot(wb, delta_b, preferred_element_type=F32)
    grad_a = lax.dot_general(nodes, delta_a, NT, preferred_element_type=F32)
    grad_b = lax.dot_general(nodes, delta_b, NT, preferred_element_type=F32)
    for d in range(8):
        out_ref[d, 0:32, :] = hidden[32 * d : 32 * d + 32].astype(BF16)
        out_ref[d, 32:64, :] = grad_a[32 * d : 32 * d + 32].astype(BF16)
        part = grad_b[32 * d : 32 * d + 32, :64]
        out_ref[d, 64:80, :] = jnp.concatenate([part[0:16], part[16:32]], axis=1).astype(BF16)


def backward_kernel(
    count_ref, rows_ref, cols_ref, got_ref, tiles_ref, out_ref, total, count, rows, cols, sems
):
    blocks = total.shape[0] - 1
    small = scalars((count_ref, rows_ref, cols_ref), (count, rows, cols), sems)
    total[...] = jnp.zeros_like(total)
    grad_a = got_ref[0, 32:64, :].astype(F32)
    grad_b = got_ref[0, 64:80, :].astype(F32)
    for d in range(1, 8):
        grad_a = grad_a + got_ref[d, 32:64, :].astype(F32)
        grad_b = grad_b + got_ref[d, 64:80, :].astype(F32)
    packed = jnp.concatenate(
        [
            jnp.concatenate([grad_a[0:16], grad_a[16:32]], axis=1),
            jnp.concatenate([grad_b[0:8], grad_b[8:16]], axis=1),
        ],
        axis=0,
    )
    for copy in small:
        copy.wait()

    live = count[0, 0]

    @pl.loop(0, (live + STEP - 1) // STEP)
    def work(step):
        products = []
        for j in range(STEP):
            row = rows[0, step * STEP + j]
            products.append(
                jnp.dot(got_ref[row, 0:32, :], tiles_ref[step * STEP + j], preferred_element_type=F32)
            )
        for j in range(STEP):
            slot = step * STEP + j
            col = jnp.where(slot < live, cols[0, slot], blocks)
            total[col] = total[col] + products[j]

    for x in range(4):
        blocks_of = [jnp.concatenate([total[2 * p], total[2 * p + 1]], axis=1) for p in range(4 * x, 4 * x + 4)]
        out_ref[x] = jnp.concatenate([*blocks_of, packed], axis=0).astype(BF16)


def sum_kernel(got_ref, out_ref):
    sums = got_ref[0].astype(F32)
    for x in range(1, 4):
        sums = sums + got_ref[x].astype(F32)
    for z in range(4):
        out_ref[z] = jnp.concatenate([sums[32 * z : 32 * z + 32], sums[128:152]], axis=0).astype(BF16)


def final_kernel(got_ref, weight_ref, feature_ref):
    sums = got_ref[0].astype(F32)
    for peer in range(1, 4):
        sums = sums + got_ref[peer].astype(F32)
    feature_ref[...] = sums[0:32]
    grad_a = sums[32:48]
    grad_b = sums[48:56]
    weight_ref[0:16, 0:TILE] = grad_a[:, 0:TILE]
    weight_ref[16:32, 0:TILE] = grad_a[:, TILE:]
    for part in range(2):
        rows = grad_b[:, part * TILE : part * TILE + TILE]
        weight_ref[8 * part : 8 * part + 8, TILE:] = rows[:, 0:44]
        weight_ref[16 + 8 * part : 24 + 8 * part, TILE:] = rows[:, 64:108]


def body(features, weight, tile_values, tile_rows, tile_cols, tile_count, labels):
    shape = jax.ShapeDtypeStruct
    vmem = pl.BlockSpec(memory_space=pltpu.VMEM)
    far = pl.BlockSpec(memory_space=pltpu.MemorySpace.HBM)
    slots = tile_values.shape[0]
    scratch = [
        pltpu.SMEM((1, TILE), jnp.int32),
        pltpu.SMEM((1, slots), jnp.int32),
        pltpu.SMEM((1, slots), jnp.int32),
        pltpu.SemaphoreType.DMA((3,)),
    ]
    params = pltpu.CompilerParams(vmem_limit_bytes=16 * 2**20)
    rows = tile_rows.reshape(1, slots)
    cols = tile_cols.reshape(1, slots)
    four, count = pl.pallas_call(
        first_kernel,
        in_specs=[pl.BlockSpec(memory_space=pltpu.MemorySpace.SMEM), vmem],
        out_specs=(vmem, vmem),
        out_shape=(shape((4, *features.shape), BF16), shape((1, TILE), jnp.int32)),
        compiler_params=params,
    )(tile_count, features)
    near = lax.all_to_all(four, "zh", 0, 0, tiled=True)
    spread = pl.pallas_call(
        spread_kernel,
        in_specs=[vmem, far],
        out_specs=vmem,
        out_shape=shape((4, *near.shape), BF16),
        compiler_params=params,
        cost_estimate=pl.CostEstimate(flops=10**10, bytes_accessed=0, transcendentals=0),
    )(near, count)
    source = lax.all_to_all(spread, "x", 0, 0, tiled=True).reshape(16, *features.shape)
    sent = pl.pallas_call(
        forward_kernel,
        in_specs=[far, far, far, vmem, vmem, vmem, vmem],
        out_specs=vmem,
        out_shape=shape((4, 8, 48, TILE), BF16),
        scratch_shapes=[pltpu.VMEM((9, 32, TILE), F32), *scratch],
        compiler_params=params,
    )(count, rows, cols, source, weight, labels.reshape(1, -1), tile_values)
    got = lax.all_to_all(sent.reshape(32, 48, TILE), ("zl", "y", "core"), 0, 0, tiled=True)
    back = pl.pallas_call(
        middle_kernel,
        in_specs=[vmem],
        out_specs=vmem,
        out_shape=shape((8, 80, TILE), BF16),
        scratch_shapes=[pltpu.VMEM((256, TILE), BF16)] * 3,
        compiler_params=params,
        cost_estimate=pl.CostEstimate(flops=10**10, bytes_accessed=0, transcendentals=0),
    )(got)
    grads = lax.all_to_all(back, DEPTH, 0, 0, tiled=True)
    parts = pl.pallas_call(
        backward_kernel,
        in_specs=[far, far, far, vmem, vmem],
        out_specs=vmem,
        out_shape=shape((4, 152, 256), BF16),
        scratch_shapes=[pltpu.VMEM((33, 32, TILE), F32), *scratch],
        compiler_params=params,
    )(count, rows, cols, grads, tile_values)
    lines = lax.all_to_all(parts, "x", 0, 0, tiled=True)
    summed = pl.pallas_call(
        sum_kernel,
        in_specs=[vmem],
        out_specs=vmem,
        out_shape=shape((4, 56, 256), BF16),
        compiler_params=params,
    )(lines)
    ours = lax.all_to_all(summed, "zh", 0, 0, tiled=True)
    return pl.pallas_call(
        final_kernel,
        in_specs=[vmem],
        out_specs=(vmem, vmem),
        out_shape=(shape((32, 172), F32), shape((32, 256), F32)),
        compiler_params=params,
    )(ours)


def solution(mesh):
    fine = Mesh(mesh.devices.reshape(4, 4, 4, 4, 2), AXES)
    tiled = ("x", "zh", "zl")
    return jax.shard_map(
        body,
        mesh=fine,
        in_specs=(
            P(DEPTH, ("zl", "x", "zh")),
            P(DEPTH, None),
            P(tiled, None, None),
            P(tiled),
            P(tiled),
            P(tiled),
            P(tiled),
        ),
        out_specs=(P(DEPTH, None), P(DEPTH, ("zl", "x", "zh"))),
        check_vma=False,
    )
```

```python
import jax
import jax.numpy as jnp
from jax import lax
from jax.experimental import pallas as pl
from jax.experimental.pallas import tpu as pltpu
from jax.sharding import Mesh
from jax.sharding import PartitionSpec as P

TILE = 128
STEP = 64
AXES = ("x", "zh", "zl", "y", "core")
DEPTH = ("y", "core")
F32 = jnp.float32
BF16 = jnp.bfloat16
NT = (((1,), (1,)), ((), ()))
TN = (((0,), (0,)), ((), ()))


def first_kernel(count_ref, own_ref, out_ref, count_out_ref):
    for z in range(4):
        out_ref[z] = own_ref[...]
    count_out_ref[...] = jnp.full(count_out_ref.shape, count_ref[0], jnp.int32)


def spread_kernel(near_ref, count_ref, out_ref):
    for x in range(4):
        out_ref[x] = near_ref[...]


def scalars(refs, held, sems):
    copies = [pltpu.make_async_copy(src, dst, sems.at[i]) for i, (src, dst) in enumerate(zip(refs, held))]
    for copy in copies:
        copy.start()
    return copies


def packed_rows(weight_ref, labels_ref, half):
    me = lax.axis_index("zl")
    weight = weight_ref[...].astype(F32)
    classes = weight.shape[1]
    mine = weight[0:8]
    for z in range(1, 4):
        mine = jnp.where(me == z, weight[8 * z : 8 * z + 8], mine)
    labels = labels_ref[:, half * TILE : half * TILE + TILE].astype(F32)
    rest = jnp.concatenate([mine[:, TILE:], jnp.zeros((8, 64 - (classes - TILE)), F32)], axis=1)
    both = jnp.concatenate([labels[:, :64], labels[:, 64:], jnp.zeros((6, 64), F32)], axis=0)
    return jnp.concatenate([mine[:, :TILE], jnp.concatenate([rest, both], axis=1)], axis=0).astype(BF16)


def forward_kernel(
    count_ref, rows_ref, cols_ref, source_ref, weight_ref, labels_ref, tiles_ref, out_ref,
    total, count, rows, cols, sems,
):
    blocks = total.shape[0] - 1
    small = scalars((count_ref, rows_ref, cols_ref), (count, rows, cols), sems)
    total[...] = jnp.zeros_like(total)
    extra = [packed_rows(weight_ref, labels_ref, half) for half in range(2)]
    for copy in small:
        copy.wait()
    live = count[0, 0]

    @pl.loop(0, (live + STEP - 1) // STEP)
    def work(step):
        products = []
        for j in range(STEP):
            col = cols[0, step * STEP + j]
            lanes = pl.ds(pl.multiple_of((col % 2) * TILE, TILE), TILE)
            products.append(
                lax.dot_general(
                    tiles_ref[step * STEP + j], source_ref[col // 2, :, lanes], NT, preferred_element_type=F32
                )
            )
        for j in range(STEP):
            slot = step * STEP + j
            row = jnp.where(slot < live, rows[0, slot], blocks)
            total[row] = total[row] + products[j]

    for d in range(blocks):
        block = jnp.concatenate([total[d].T.astype(BF16), extra[d % 2]], axis=0)
        for z in range(4):
            out_ref[z, d] = block


def middle_kernel(got_ref, out_ref, agg, weight_a, weight_b):
    me = lax.axis_index(DEPTH)
    for d in range(8):
        sums = got_ref[d, 0:32, :].astype(F32)
        for z in range(1, 4):
            sums = sums + got_ref[8 * z + d, 0:32, :].astype(F32)
        agg[32 * d : 32 * d + 32, :] = sums.astype(BF16)
        pieces = [got_ref[8 * z + d, 32:48, :].astype(F32) for z in range(4)]
        weight_a[32 * d : 32 * d + 32, :] = jnp.concatenate([p[0:8] for p in pieces], axis=0).astype(BF16)
        weight_b[32 * d : 32 * d + 32, :] = jnp.concatenate([p[8:16] for p in pieces], axis=0).astype(BF16)
    carrier = got_ref[(me // 2) * 8, 32:48, :].astype(F32)
    labels = jnp.concatenate([carrier[8:9, 64:], carrier[9:10, 64:]], axis=1)
    nodes = agg[...]
    wa = weight_a[...]
    wb = weight_b[...]
    ids = lax.broadcasted_iota(jnp.int32, (TILE, TILE), 0).astype(F32)
    exp_a = jnp.exp(lax.dot_general(wa, nodes, TN, preferred_element_type=F32))
    logit_b = lax.dot_general(wb, nodes, TN, preferred_element_type=F32)
    valid = ids < 172 - TILE
    exp_b = jnp.where(valid, jnp.exp(jnp.where(valid, logit_b, 0.0)), 0.0)
    whole = jnp.sum(exp_a, axis=0, keepdims=True) + jnp.sum(exp_b, axis=0, keepdims=True)
    delta_a = (exp_a / whole - jnp.where(ids == labels, 1.0, 0.0)).astype(BF16)
    delta_b = (exp_b / whole - jnp.where(ids + TILE == labels, 1.0, 0.0)).astype(BF16)
    hidden = jnp.dot(wa, delta_a, preferred_element_type=F32) + jnp.dot(wb, delta_b, preferred_element_type=F32)
    grad_a = lax.dot_general(nodes, delta_a, NT, preferred_element_type=F32)
    grad_b = lax.dot_general(nodes, delta_b, NT, preferred_element_type=F32)
    for d in range(8):
        out_ref[d, 0:32, :] = hidden[32 * d : 32 * d + 32].astype(BF16)
        out_ref[d, 32:64, :] = grad_a[32 * d : 32 * d + 32].astype(BF16)
        part = grad_b[32 * d : 32 * d + 32, :64]
        out_ref[d, 64:80, :] = jnp.concatenate([part[0:16], part[16:32]], axis=1).astype(BF16)


def backward_kernel(
    count_ref, rows_ref, cols_ref, got_ref, tiles_ref, out_ref, total, count, rows, cols, sems
):
    blocks = total.shape[0] - 1
    small = scalars((count_ref, rows_ref, cols_ref), (count, rows, cols), sems)
    total[...] = jnp.zeros_like(total)
    grad_a = got_ref[0, 32:64, :].astype(F32)
    grad_b = got_ref[0, 64:80, :].astype(F32)
    for d in range(1, 8):
        grad_a = grad_a + got_ref[d, 32:64, :].astype(F32)
        grad_b = grad_b + got_ref[d, 64:80, :].astype(F32)
    packed = jnp.concatenate(
        [
            jnp.concatenate([grad_a[0:16], grad_a[16:32]], axis=1),
            jnp.concatenate([grad_b[0:8], grad_b[8:16]], axis=1),
        ],
        axis=0,
    )
    for copy in small:
        copy.wait()

    live = count[0, 0]

    @pl.loop(0, (live + STEP - 1) // STEP)
    def work(step):
        products = []
        for j in range(STEP):
            row = rows[0, step * STEP + j]
            products.append(
                jnp.dot(got_ref[row, 0:32, :], tiles_ref[step * STEP + j], preferred_element_type=F32)
            )
        for j in range(STEP):
            slot = step * STEP + j
            col = jnp.where(slot < live, cols[0, slot], blocks)
            total[col] = total[col] + products[j]

    for x in range(4):
        blocks_of = [jnp.concatenate([total[2 * p], total[2 * p + 1]], axis=1) for p in range(4 * x, 4 * x + 4)]
        out_ref[x] = jnp.concatenate([*blocks_of, packed], axis=0).astype(BF16)


def sum_kernel(got_ref, out_ref):
    sums = got_ref[0].astype(F32)
    for x in range(1, 4):
        sums = sums + got_ref[x].astype(F32)
    for z in range(4):
        out_ref[z] = jnp.concatenate([sums[32 * z : 32 * z + 32], sums[128:152]], axis=0).astype(BF16)


def final_kernel(got_ref, weight_ref, feature_ref):
    sums = got_ref[0].astype(F32)
    for peer in range(1, 4):
        sums = sums + got_ref[peer].astype(F32)
    feature_ref[...] = sums[0:32]
    grad_a = sums[32:48]
    grad_b = sums[48:56]
    weight_ref[0:16, 0:TILE] = grad_a[:, 0:TILE]
    weight_ref[16:32, 0:TILE] = grad_a[:, TILE:]
    for part in range(2):
        rows = grad_b[:, part * TILE : part * TILE + TILE]
        weight_ref[8 * part : 8 * part + 8, TILE:] = rows[:, 0:44]
        weight_ref[16 + 8 * part : 24 + 8 * part, TILE:] = rows[:, 64:108]


def body(features, weight, tile_values, tile_rows, tile_cols, tile_count, labels):
    shape = jax.ShapeDtypeStruct
    vmem = pl.BlockSpec(memory_space=pltpu.VMEM)
    far = pl.BlockSpec(memory_space=pltpu.MemorySpace.HBM)
    slots = tile_values.shape[0]
    scratch = [
        pltpu.SMEM((1, TILE), jnp.int32),
        pltpu.SMEM((1, slots), jnp.int32),
        pltpu.SMEM((1, slots), jnp.int32),
        pltpu.SemaphoreType.DMA((3,)),
    ]
    params = pltpu.CompilerParams(vmem_limit_bytes=16 * 2**20)
    rows = tile_rows.reshape(1, slots)
    cols = tile_cols.reshape(1, slots)
    four, count = pl.pallas_call(
        first_kernel,
        in_specs=[pl.BlockSpec(memory_space=pltpu.MemorySpace.SMEM), vmem],
        out_specs=(vmem, vmem),
        out_shape=(shape((4, *features.shape), BF16), shape((1, TILE), jnp.int32)),
        compiler_params=params,
    )(tile_count, features)
    near = lax.all_to_all(four, "zh", 0, 0, tiled=True)
    spread = pl.pallas_call(
        spread_kernel,
        in_specs=[vmem, far],
        out_specs=vmem,
        out_shape=shape((4, *near.shape), BF16),
        compiler_params=params,
        cost_estimate=pl.CostEstimate(flops=10**10, bytes_accessed=0, transcendentals=0),
    )(near, count)
    source = lax.all_to_all(spread, "x", 0, 0, tiled=True).reshape(16, *features.shape)
    sent = pl.pallas_call(
        forward_kernel,
        in_specs=[far, far, far, vmem, vmem, vmem, vmem],
        out_specs=vmem,
        out_shape=shape((4, 8, 48, TILE), BF16),
        scratch_shapes=[pltpu.VMEM((9, TILE, 32), F32), *scratch],
        compiler_params=params,
    )(count, rows, cols, source, weight, labels.reshape(1, -1), tile_values)
    got = lax.all_to_all(sent.reshape(32, 48, TILE), ("zl", "y", "core"), 0, 0, tiled=True)
    back = pl.pallas_call(
        middle_kernel,
        in_specs=[vmem],
        out_specs=vmem,
        out_shape=shape((8, 80, TILE), BF16),
        scratch_shapes=[pltpu.VMEM((256, TILE), BF16)] * 3,
        compiler_params=params,
        cost_estimate=pl.CostEstimate(flops=10**10, bytes_accessed=0, transcendentals=0),
    )(got)
    grads = lax.all_to_all(back, DEPTH, 0, 0, tiled=True)
    parts = pl.pallas_call(
        backward_kernel,
        in_specs=[far, far, far, vmem, vmem],
        out_specs=vmem,
        out_shape=shape((4, 152, 256), BF16),
        scratch_shapes=[pltpu.VMEM((33, 32, TILE), F32), *scratch],
        compiler_params=params,
    )(count, rows, cols, grads, tile_values)
    lines = lax.all_to_all(parts, "x", 0, 0, tiled=True)
    summed = pl.pallas_call(
        sum_kernel,
        in_specs=[vmem],
        out_specs=vmem,
        out_shape=shape((4, 56, 256), BF16),
        compiler_params=params,
    )(lines)
    ours = lax.all_to_all(summed, "zh", 0, 0, tiled=True)
    return pl.pallas_call(
        final_kernel,
        in_specs=[vmem],
        out_specs=(vmem, vmem),
        out_shape=(shape((32, 172), F32), shape((32, 256), F32)),
        compiler_params=params,
    )(ours)


def solution(mesh):
    fine = Mesh(mesh.devices.reshape(4, 4, 4, 4, 2), AXES)
    tiled = ("x", "zh", "zl")
    return jax.shard_map(
        body,
        mesh=fine,
        in_specs=(
            P(DEPTH, ("zl", "x", "zh")),
            P(DEPTH, None),
            P(tiled, None, None),
            P(tiled),
            P(tiled),
            P(tiled),
            P(tiled),
        ),
        out_specs=(P(DEPTH, None), P(DEPTH, ("zl", "x", "zh"))),
        check_vma=False,
    )
```

```python
import jax
import jax.numpy as jnp
from jax import lax
from jax.experimental import pallas as pl
from jax.experimental.pallas import tpu as pltpu
from jax.sharding import Mesh
from jax.sharding import PartitionSpec as P

TILE = 128
STEP = 64
AXES = ("x", "zh", "zl", "y", "core")
DEPTH = ("y", "core")
F32 = jnp.float32
BF16 = jnp.bfloat16
NT = (((1,), (1,)), ((), ()))
TN = (((0,), (0,)), ((), ()))


def spread_kernel(count_ref, near_ref, out_ref, count_out_ref):
    for x in range(4):
        out_ref[x] = near_ref[...]
    count_out_ref[...] = jnp.full(count_out_ref.shape, count_ref[0], jnp.int32)


def scalars(refs, held, sems):
    copies = [pltpu.make_async_copy(src, dst, sems.at[i]) for i, (src, dst) in enumerate(zip(refs, held))]
    for copy in copies:
        copy.start()
    return copies


def packed_rows(weight_ref, labels_ref, half):
    me = lax.axis_index("zl")
    weight = weight_ref[...].astype(F32)
    classes = weight.shape[1]
    mine = weight[0:8]
    for z in range(1, 4):
        mine = jnp.where(me == z, weight[8 * z : 8 * z + 8], mine)
    labels = labels_ref[:, half * TILE : half * TILE + TILE].astype(F32)
    rest = jnp.concatenate([mine[:, TILE:], jnp.zeros((8, 64 - (classes - TILE)), F32)], axis=1)
    both = jnp.concatenate([labels[:, :64], labels[:, 64:], jnp.zeros((6, 64), F32)], axis=0)
    return jnp.concatenate([mine[:, :TILE], jnp.concatenate([rest, both], axis=1)], axis=0).astype(BF16)


def forward_kernel(
    count_ref, rows_ref, cols_ref, source_ref, weight_ref, labels_ref, tiles_ref, out_ref,
    total, count, rows, cols, sems,
):
    blocks = total.shape[0] - 1
    small = scalars((count_ref, rows_ref, cols_ref), (count, rows, cols), sems)
    total[...] = jnp.zeros_like(total)
    extra = [packed_rows(weight_ref, labels_ref, half) for half in range(2)]
    for copy in small:
        copy.wait()
    live = count[0, 0]

    @pl.loop(0, (live + STEP - 1) // STEP)
    def work(step):
        products = []
        for j in range(STEP):
            col = cols[0, step * STEP + j]
            lanes = pl.ds(pl.multiple_of((col % 2) * TILE, TILE), TILE)
            products.append(
                lax.dot_general(
                    tiles_ref[step * STEP + j], source_ref[col // 2, :, lanes], NT, preferred_element_type=F32
                )
            )
        for j in range(STEP):
            slot = step * STEP + j
            row = jnp.where(slot < live, rows[0, slot], blocks)
            total[row] = total[row] + products[j]

    for d in range(blocks):
        block = jnp.concatenate([total[d].T.astype(BF16), extra[d % 2]], axis=0)
        for z in range(4):
            out_ref[z, d] = block


def middle_kernel(got_ref, out_ref, agg, weight_a, weight_b):
    me = lax.axis_index(DEPTH)
    for d in range(8):
        sums = got_ref[d, 0:32, :].astype(F32)
        for z in range(1, 4):
            sums = sums + got_ref[8 * z + d, 0:32, :].astype(F32)
        agg[32 * d : 32 * d + 32, :] = sums.astype(BF16)
        pieces = [got_ref[8 * z + d, 32:48, :].astype(F32) for z in range(4)]
        weight_a[32 * d : 32 * d + 32, :] = jnp.concatenate([p[0:8] for p in pieces], axis=0).astype(BF16)
        weight_b[32 * d : 32 * d + 32, :] = jnp.concatenate([p[8:16] for p in pieces], axis=0).astype(BF16)
    carrier = got_ref[(me // 2) * 8, 32:48, :].astype(F32)
    labels = jnp.concatenate([carrier[8:9, 64:], carrier[9:10, 64:]], axis=1)
    nodes = agg[...]
    wa = weight_a[...]
    wb = weight_b[...]
    ids = lax.broadcasted_iota(jnp.int32, (TILE, TILE), 0).astype(F32)
    exp_a = jnp.exp(lax.dot_general(wa, nodes, TN, preferred_element_type=F32))
    logit_b = lax.dot_general(wb, nodes, TN, preferred_element_type=F32)
    valid = ids < 172 - TILE
    exp_b = jnp.where(valid, jnp.exp(jnp.where(valid, logit_b, 0.0)), 0.0)
    whole = jnp.sum(exp_a, axis=0, keepdims=True) + jnp.sum(exp_b, axis=0, keepdims=True)
    delta_a = (exp_a / whole - jnp.where(ids == labels, 1.0, 0.0)).astype(BF16)
    delta_b = (exp_b / whole - jnp.where(ids + TILE == labels, 1.0, 0.0)).astype(BF16)
    hidden = jnp.dot(wa, delta_a, preferred_element_type=F32) + jnp.dot(wb, delta_b, preferred_element_type=F32)
    grad_a = lax.dot_general(nodes, delta_a, NT, preferred_element_type=F32)
    grad_b = lax.dot_general(nodes, delta_b, NT, preferred_element_type=F32)
    for d in range(8):
        out_ref[d, 0:32, :] = hidden[32 * d : 32 * d + 32].astype(BF16)
        out_ref[d, 32:64, :] = grad_a[32 * d : 32 * d + 32].astype(BF16)
        part = grad_b[32 * d : 32 * d + 32, :64]
        out_ref[d, 64:80, :] = jnp.concatenate([part[0:16], part[16:32]], axis=1).astype(BF16)


def backward_kernel(
    count_ref, rows_ref, cols_ref, got_ref, tiles_ref, out_ref, total, count, rows, cols, sems
):
    blocks = total.shape[0] - 1
    small = scalars((count_ref, rows_ref, cols_ref), (count, rows, cols), sems)
    total[...] = jnp.zeros_like(total)
    grad_a = got_ref[0, 32:64, :].astype(F32)
    grad_b = got_ref[0, 64:80, :].astype(F32)
    for d in range(1, 8):
        grad_a = grad_a + got_ref[d, 32:64, :].astype(F32)
        grad_b = grad_b + got_ref[d, 64:80, :].astype(F32)
    packed = jnp.concatenate(
        [
            jnp.concatenate([grad_a[0:16], grad_a[16:32]], axis=1),
            jnp.concatenate([grad_b[0:8], grad_b[8:16]], axis=1),
        ],
        axis=0,
    )
    for copy in small:
        copy.wait()

    live = count[0, 0]

    @pl.loop(0, (live + STEP - 1) // STEP)
    def work(step):
        products = []
        for j in range(STEP):
            row = rows[0, step * STEP + j]
            products.append(
                jnp.dot(got_ref[row, 0:32, :], tiles_ref[step * STEP + j], preferred_element_type=F32)
            )
        for j in range(STEP):
            slot = step * STEP + j
            col = jnp.where(slot < live, cols[0, slot], blocks)
            total[col] = total[col] + products[j]

    for x in range(4):
        blocks_of = [jnp.concatenate([total[2 * p], total[2 * p + 1]], axis=1) for p in range(4 * x, 4 * x + 4)]
        out_ref[x] = jnp.concatenate([*blocks_of, packed], axis=0).astype(BF16)


def sum_kernel(got_ref, out_ref):
    sums = got_ref[0].astype(F32)
    for x in range(1, 4):
        sums = sums + got_ref[x].astype(F32)
    for z in range(4):
        out_ref[z] = jnp.concatenate([sums[32 * z : 32 * z + 32], sums[128:152]], axis=0).astype(BF16)


def final_kernel(got_ref, weight_ref, feature_ref):
    sums = got_ref[0].astype(F32)
    for peer in range(1, 4):
        sums = sums + got_ref[peer].astype(F32)
    feature_ref[...] = sums[0:32]
    grad_a = sums[32:48]
    grad_b = sums[48:56]
    weight_ref[0:16, 0:TILE] = grad_a[:, 0:TILE]
    weight_ref[16:32, 0:TILE] = grad_a[:, TILE:]
    for part in range(2):
        rows = grad_b[:, part * TILE : part * TILE + TILE]
        weight_ref[8 * part : 8 * part + 8, TILE:] = rows[:, 0:44]
        weight_ref[16 + 8 * part : 24 + 8 * part, TILE:] = rows[:, 64:108]


def body(features, weight, tile_values, tile_rows, tile_cols, tile_count, labels):
    shape = jax.ShapeDtypeStruct
    vmem = pl.BlockSpec(memory_space=pltpu.VMEM)
    far = pl.BlockSpec(memory_space=pltpu.MemorySpace.HBM)
    slots = tile_values.shape[0]
    scratch = [
        pltpu.SMEM((1, TILE), jnp.int32),
        pltpu.SMEM((1, slots), jnp.int32),
        pltpu.SMEM((1, slots), jnp.int32),
        pltpu.SemaphoreType.DMA((3,)),
    ]
    params = pltpu.CompilerParams(vmem_limit_bytes=16 * 2**20)
    rows = tile_rows.reshape(1, slots)
    cols = tile_cols.reshape(1, slots)
    near = lax.all_gather(features, "zh", axis=0)
    spread, count = pl.pallas_call(
        spread_kernel,
        in_specs=[pl.BlockSpec(memory_space=pltpu.MemorySpace.SMEM), vmem],
        out_specs=(vmem, vmem),
        out_shape=(shape((4, *near.shape), BF16), shape((1, TILE), jnp.int32)),
        compiler_params=params,
        cost_estimate=pl.CostEstimate(flops=10**10, bytes_accessed=0, transcendentals=0),
    )(tile_count, near)
    source = lax.all_to_all(spread, "x", 0, 0, tiled=True).reshape(16, *features.shape)
    sent = pl.pallas_call(
        forward_kernel,
        in_specs=[far, far, far, vmem, vmem, vmem, vmem],
        out_specs=vmem,
        out_shape=shape((4, 8, 48, TILE), BF16),
        scratch_shapes=[pltpu.VMEM((9, TILE, 32), F32), *scratch],
        compiler_params=params,
    )(count, rows, cols, source, weight, labels.reshape(1, -1), tile_values)
    got = lax.all_to_all(sent.reshape(32, 48, TILE), ("zl", "y", "core"), 0, 0, tiled=True)
    back = pl.pallas_call(
        middle_kernel,
        in_specs=[vmem],
        out_specs=vmem,
        out_shape=shape((8, 80, TILE), BF16),
        scratch_shapes=[pltpu.VMEM((256, TILE), BF16)] * 3,
        compiler_params=params,
        cost_estimate=pl.CostEstimate(flops=10**10, bytes_accessed=0, transcendentals=0),
    )(got)
    grads = lax.all_to_all(back, DEPTH, 0, 0, tiled=True)
    parts = pl.pallas_call(
        backward_kernel,
        in_specs=[far, far, far, vmem, vmem],
        out_specs=vmem,
        out_shape=shape((4, 152, 256), BF16),
        scratch_shapes=[pltpu.VMEM((33, 32, TILE), F32), *scratch],
        compiler_params=params,
    )(count, rows, cols, grads, tile_values)
    lines = lax.all_to_all(parts, "x", 0, 0, tiled=True)
    summed = pl.pallas_call(
        sum_kernel,
        in_specs=[vmem],
        out_specs=vmem,
        out_shape=shape((4, 56, 256), BF16),
        compiler_params=params,
    )(lines)
    ours = lax.all_to_all(summed, "zh", 0, 0, tiled=True)
    return pl.pallas_call(
        final_kernel,
        in_specs=[vmem],
        out_specs=(vmem, vmem),
        out_shape=(shape((32, 172), F32), shape((32, 256), F32)),
        compiler_params=params,
    )(ours)


def solution(mesh):
    fine = Mesh(mesh.devices.reshape(4, 4, 4, 4, 2), AXES)
    tiled = ("x", "zh", "zl")
    return jax.shard_map(
        body,
        mesh=fine,
        in_specs=(
            P(DEPTH, ("zl", "x", "zh")),
            P(DEPTH, None),
            P(tiled, None, None),
            P(tiled),
            P(tiled),
            P(tiled),
            P(tiled),
        ),
        out_specs=(P(DEPTH, None), P(DEPTH, ("zl", "x", "zh"))),
        check_vma=False,
    )
```
